512 devices in a mesh: tm: 8 (over y), rows: 8 (over z_lo, core), cols: 8 (over z_hi, x).
Axes of the slice: x: 4, y: 8, z: 8 (z_hi: 2, z_lo: 4; z = z_hi * 4 + z_lo), core: 2. Of those that a mesh axis runs over, the one named last changes fastest.
Arguments:
- latent: bfloat16 [24, 16, 64, 384], P('tm', 'rows', 'cols'), may hold values from -6 to 6
- cotangent: bfloat16 [24, 32, 128, 192], P('tm', 'rows', 'cols'), may hold values from -6 to 6
- resample_weight: bfloat16 [3, 3, 384, 192], replicated, may hold values from -0.109375 to 0.109375
- conv_weight: bfloat16 [3, 3, 3, 192, 192], replicated, may hold values from -0.078125 to 0.078125
- norm_gain: float32 [192], replicated, may hold values from 0.1 to 1.9
Outputs:
- grad_input: bfloat16 [24, 16, 64, 384], P('tm', 'rows', 'cols')
- grad_resample: float32 [663552], P(('tm', 'rows', 'cols'))
- grad_conv: float32 [995328], P(('tm', 'rows', 'cols'))
- grad_gain: float32 [192], replicated
The draws below stay inside these ranges and needn't reach their ends.
All inputs are finite; a program needn't handle non-finite values.
Results may differ from the reference program's by a relative error of at most 0.013.
Values may be sent and summed in bfloat16 or wider, within the bound.
A program may use at most 128 MiB of HBM per device.

```python
import jax
import jax.numpy as jnp
from jax import lax

CIN = 384
CH = 192
FRAMES = 24
HLO = 16
WLO = 64
HEIGHT = 32
WIDTH = 128


def block_scale(rng, shape, split, smallest, largest):
    def one(axis_at, parts):
        draws = jax.random.uniform(jax.random.fold_in(jax.random.fold_in(rng, 6), axis_at), (parts,), jnp.float32, smallest / len(split), largest / len(split))
        return jnp.repeat(jnp.exp(draws), shape[axis_at] // parts).reshape((-1,) + (1,) * (len(shape) - axis_at - 1))

    gain = one(*split[0])
    for cut in split[1:]:
        gain = gain * one(*cut)
    return gain


def noise(rng, dims, scale, reach, shards=(), held_as=jnp.bfloat16):
    drawn = scale * jax.random.normal(rng, dims, jnp.float32)
    if shards:
        drawn = drawn * block_scale(rng, dims, shards, -0.22, 0.18)
    return jnp.clip(drawn, -reach, reach).astype(held_as)


def setup_inputs(seed: int = 0) -> dict:
    arg_keys = jax.random.split(jax.random.key(seed), 6)
    return {
        "latent": noise(arg_keys[0], (FRAMES, HLO, WLO, CIN), 1.0, 6.0, ((0, 8), (1, 8), (2, 8))),
        "cotangent": noise(arg_keys[1], (FRAMES, HEIGHT, WIDTH, CH), 1.0, 6.0, ((0, 8), (1, 8), (2, 8))),
        "resample_weight": noise(arg_keys[2], (3, 3, CIN, CH), (9 * CIN) ** -0.5, 0.109375),
        "conv_weight": noise(arg_keys[3], (3, 3, 3, CH, CH), (27 * CH) ** -0.5, 0.078125),
        "norm_gain": jnp.clip(1.0 + 0.18 * jax.random.normal(arg_keys[4], (CH,), jnp.float32), 0.1, 1.9),
    }


EPSILON = 1e-06

def upsample(values):
    return jnp.repeat(jnp.repeat(values, 2, axis=1), 2, axis=2)

def reference(latent, cotangent, resample_weight, conv_weight, norm_gain):
    dims_two = ('NHWC', 'HWIO', 'NHWC')
    dims_three = ('NDHWC', 'DHWIO', 'NDHWC')
    lifted = upsample(latent)
    resampled = lax.conv_general_dilated(lifted, resample_weight, (1, 1), ((1, 1), (1, 1)), dimension_numbers=dims_two, preferred_element_type=jnp.float32).astype(jnp.bfloat16)
    z_float = resampled.astype(jnp.float32)
    inverse = lax.rsqrt(lax.optimization_barrier(jnp.mean(z_float * z_float, axis=-1, keepdims=True)) + EPSILON)
    normed = z_float * inverse
    scaled = normed * norm_gain
    sigma = jax.nn.sigmoid(scaled)
    hidden = (scaled * sigma).astype(jnp.bfloat16)
    flipped = jnp.transpose(jnp.flip(conv_weight, (0, 1, 2)), (0, 1, 2, 4, 3))
    hidden_grad = lax.conv_general_dilated(cotangent[None], flipped, (1, 1, 1), ((0, 2), (1, 1), (1, 1)), dimension_numbers=dims_three, preferred_element_type=jnp.float32)[0]
    scaled_grad = hidden_grad * sigma * (1.0 + scaled * (1.0 - sigma))
    grad_gain = lax.optimization_barrier(jnp.sum(scaled_grad * normed, axis=(0, 1, 2)))
    normed_grad = scaled_grad * norm_gain
    delta = (inverse * (normed_grad - normed * lax.optimization_barrier(jnp.mean(normed_grad * normed, axis=-1, keepdims=True)))).astype(jnp.bfloat16)
    flip_two = jnp.transpose(jnp.flip(resample_weight, (0, 1)), (0, 1, 3, 2))
    lifted_grad = lax.conv_general_dilated(delta, flip_two, (1, 1), ((1, 1), (1, 1)), dimension_numbers=dims_two, preferred_element_type=jnp.float32)
    frames, height, width = (cotangent.shape[0], cotangent.shape[1], cotangent.shape[2])
    grad_input = lifted_grad.reshape(frames, height // 2, 2, width // 2, 2, -1).sum(axis=(2, 4)).astype(jnp.bfloat16)
    hidden_pad = jnp.pad(hidden, ((2, 0), (1, 1), (1, 1), (0, 0))).astype(jnp.float32)
    grad_float = cotangent.astype(jnp.float32)
    conv_terms = []
    for step_t in range(3):
        for step_y in range(3):
            for step_x in range(3):
                window = hidden_pad[step_t:step_t + frames, step_y:step_y + height, step_x:step_x + width]
                conv_terms.append(jnp.einsum('thwc,thwo->co', window, grad_float))
    grad_conv = jnp.stack(conv_terms).reshape(-1)
    lifted_pad = jnp.pad(lifted, ((0, 0), (1, 1), (1, 1), (0, 0))).astype(jnp.float32)
    delta_float = delta.astype(jnp.float32)
    resample_terms = []
    for step_y in range(3):
        for step_x in range(3):
            window = lifted_pad[:, step_y:step_y + height, step_x:step_x + width]
            resample_terms.append(jnp.einsum('thwc,thwo->co', window, delta_float))
    grad_resample = jnp.stack(resample_terms).reshape(-1)
    return (grad_input, grad_resample, grad_conv, grad_gain)
```

```python
import functools

import jax
import jax.numpy as jnp
import numpy as np
from jax import lax
from jax.experimental import pallas as pl
from jax.experimental.pallas import tpu as pltpu
from jax.sharding import PartitionSpec as P

EPSILON = 1e-06
MESH = pl.DeviceIdType.MESH
BF = jnp.bfloat16
F32 = jnp.float32


def selectors():
    low = [0, 1, 1, 2, 2, 3]

    def zeros(*dims):
        return np.zeros(dims, np.float32)

    widen = zeros(96, 48)
    for t in range(3):
        for l in range(2):
            for c in range(16):
                widen[t * 32 + l * 16 + c, t * 16 + l * 8 + c // 2] = 1
    even_192, even_384 = zeros(192, 192), zeros(384, 384)
    for u in range(96):
        even_192[2 * u, u] = even_192[2 * u + 1, 96 + u] = 1
    for u in range(192):
        even_384[2 * u, u] = even_384[2 * u + 1, 192 + u] = 1
    lift, lift_rim = zeros(3, 96, 64), zeros(2, 3, 96, 16)
    cot, cot_rim = zeros(2, 96, 96), zeros(2, 5, 96, 32)
    pair, pair_rim = zeros(3, 96, 96), zeros(2, 3, 96, 32)
    for row in range(6):
        for c in range(16):
            out = row * 16 + c
            par = row * 16 + (c % 2) * 8 + c // 2
            for j in range(3):
                at = c + j - 1
                if 0 <= at < 16:
                    lift[j, out, low[row] * 16 + at] = 1
                    pair[j, par, row * 16 + at] = 1
                    if j != 1:
                        cot[j // 2, out, row * 16 + at] = 1
                else:
                    side = j // 2
                    for f in range(5):
                        cot_rim[side, f, out, f * 6 + row] = 1
                    for f in range(3):
                        lift_rim[side, f, out, f * 4 + low[row]] = 1
                        pair_rim[side, f, par, f * 6 + row] = 1
    edge_cot, edge_low = zeros(64, 480), zeros(32, 192)
    for side, col in ((0, 0), (1, 15)):
        for n in range(30):
            edge_cot[side * 32 + n, n * 16 + col] = 1
        for n in range(12):
            edge_low[side * 16 + n, n * 16 + col] = 1
    parts = (widen, even_192, even_384, lift, lift_rim, cot, cot_rim, pair, pair_rim, edge_cot, edge_low)
    return [jnp.asarray(p, BF) for p in parts]


def mm(a, b):
    return jnp.dot(a, b, preferred_element_type=F32)


def mm_nt(a, b):
    return lax.dot_general(a, b, (((1,), (1,)), ((), ())), preferred_element_type=F32)


def mm_tn(a, b):
    return lax.dot_general(a, b, (((0,), (0,)), ((), ())), preferred_element_type=F32)


def kernel(
    latent_ref, cot_ref, gain_ref, wr_hbm, wc_hbm,
    widen, even_192, even_384, lift, lift_rim, cot, cot_rim, pair, pair_rim, edge_cot, edge_low,
    gi_ref, oc_ref, or_ref, og_ref,
    wr, wc, sc, lc, lcp, hs_c, hs_l, hs_d, rim_c, rim_l, rim_d, sl, slp, xd, sd,
    fc, fr, bs_c, br_c, xs_c, xr_c, ac_c, ys_c, yr_c,
    bs_r, br_r, xs_r, xr_r, ac_r, ys_r, yr_r,
    g_core, g_x, g_y, pw_c, pw_r, ws, land, flat_c, flat_r,
    load_sem, ssem, rsem, core_s, core_r, x_s, x_r, y_s, y_r, fin_s, fin_r,
    gc_s, gc_r, gx_s, gx_r, gy_s, gy_r,
):
    y, r, c = lax.axis_index("tm"), lax.axis_index("rows"), lax.axis_index("cols")
    h, zl = r % 2, r // 2
    x, zh = c % 4, c // 4
    z = zh * 4 + zl

    def dev(dy=0, dr=0, dc=0):
        return ((y + dy + 8) % 8, (r + dr + 8) % 8, (c + dc + 8) % 8)

    partner = (y, zl * 2 + 1 - h, c)

    def peer_x(o):
        return (y, r, zh * 4 + (x + o) % 4)

    load_r = pltpu.make_async_copy(wr_hbm, wr, load_sem.at[0])
    load_c = pltpu.make_async_copy(wc_hbm, wc, load_sem.at[1])
    load_r.start()
    load_c.start()

    bar = pltpu.get_barrier_semaphore()
    sources = [dev(0, 1), dev(0, -1), dev(1, 0), dev(1, 1), dev(1, -1), dev(0, 0, 1), dev(0, 0, -1), partner]
    sources += [peer_x(o) for o in range(1, 4)] + [dev(o) for o in range(1, 8)]
    for d in sources:
        pl.semaphore_signal(bar, inc=1, device_id=d, device_id_type=MESH)
    for q in range(8):
        src = (y, 2 * (q % 4) + r // 4, (q // 4) * 4 + r % 4)

        @pl.when(jnp.logical_or(src[1] != r, src[2] != c))
        def _():
            pl.semaphore_signal(bar, inc=1, device_id=src, device_id_type=MESH)

    mine = jnp.where(r == 4 * h + x, 1, 0)

    sc[1, 0:3, 1:5] = cot_ref[...]
    own_low = latent_ref[...].astype(F32).reshape(48, 384).astype(BF)
    lc[:, 1:3] = mm(widen[...], own_low).astype(BF).reshape(3, 2, 16, 384)

    pl.semaphore_wait(bar, len(sources) + 8 - mine)

    def remote(src, dst, n, to):
        return pltpu.make_async_remote_copy(
            src_ref=src, dst_ref=dst, send_sem=ssem.at[n], recv_sem=rsem.at[n],
            device_id=to, device_id_type=MESH,
        )

    f3, f2, late = pl.ds(0, 3), pl.ds(0, 2), pl.ds(3, 2)
    first = [
        remote(sc.at[1, f3, 1], sc.at[1, f3, 5], 0, dev(0, -1)),
        remote(sc.at[1, f3, 4], sc.at[1, f3, 0], 1, dev(0, 1)),
        remote(lc.at[f3, 1], lc.at[f3, 3], 5, dev(0, -1)),
        remote(lc.at[f3, 2], lc.at[f3, 0], 6, dev(0, 1)),
        remote(sc.at[1, f2, pl.ds(1, 4)], sc.at[1, late, pl.ds(1, 4)], 2, dev(-1, 0)),
        remote(sc.at[1, f2, 1], sc.at[1, late, 5], 3, dev(-1, -1)),
        remote(sc.at[1, f2, 4], sc.at[1, late, 0], 4, dev(-1, 1)),
    ]
    for copy in first:
        copy.start()
    for copy in first:
        copy.wait()

    @pl.when(r == 0)
    def _():
        sc[1, :, 0] = jnp.zeros((5, 16, 192), BF)
        lc[:, 0] = jnp.zeros((3, 16, 384), BF)

    @pl.when(r == 7)
    def _():
        sc[1, :, 5] = jnp.zeros((5, 16, 192), BF)
        lc[:, 3] = jnp.zeros((3, 16, 384), BF)

    @pl.when(y == 7)
    def _():
        sc[1, 3:5] = jnp.zeros((2, 6, 16, 192), BF)

    low_all = lc[...].reshape(192, 384)
    hs_l[...] = mm(edge_low[...], low_all).astype(BF)
    hs_c[...] = mm(edge_cot[...], sc[1].reshape(480, 192)).astype(BF)
    second = [
        remote(hs_l.at[pl.ds(0, 16)], rim_l.at[1], 9, dev(0, 0, -1)),
        remote(hs_l.at[pl.ds(16, 16)], rim_l.at[0], 10, dev(0, 0, 1)),
        remote(hs_c.at[pl.ds(0, 32)], rim_c.at[1], 7, dev(0, 0, -1)),
        remote(hs_c.at[pl.ds(32, 32)], rim_c.at[0], 8, dev(0, 0, 1)),
    ]
    for copy in second:
        copy.start()
    lcp[...] = mm(low_all, even_384[...]).astype(BF).reshape(3, 4, 16, 384)
    load_r.wait()
    load_c.wait()
    for copy in second:
        copy.wait()

    @pl.when(c == 0)
    def _():
        rim_l[0] = jnp.zeros((16, 384), BF)
        rim_c[0] = jnp.zeros((32, 192), BF)

    @pl.when(c == 7)
    def _():
        rim_l[1] = jnp.zeros((16, 384), BF)
        rim_c[1] = jnp.zeros((32, 192), BF)

    rim_p = [mm(rim_l[s], even_384[...]).astype(BF) for s in range(2)]
    for t in range(3):
        here = lc[t].reshape(64, 384)
        here_p = lcp[t].reshape(64, 384)
        for j in range(3):
            wide, wide_p = mm(lift[j], here), mm(lift[j], here_p)
            if j != 1:
                wide += mm(lift_rim[j // 2, t], rim_l[j // 2])
                wide_p += mm(lift_rim[j // 2, t], rim_p[j // 2])
            sl[j, t] = wide.astype(BF).reshape(6, 16, 384)
            slp[j, t] = wide_p.astype(BF).reshape(6, 16, 384)

    def fwd(i, total):
        for j in range(3):
            total += mm(sl[j, :, pl.ds(i, 4)].reshape(192, 384), wr[i, j])
        return total

    z_float = lax.fori_loop(0, 3, fwd, jnp.zeros((192, 192), F32)).astype(BF).astype(F32)
    gain = gain_ref[...]
    inverse = lax.rsqrt(jnp.mean(z_float * z_float, axis=-1, keepdims=True) + EPSILON)
    normed = z_float * inverse
    scaled = normed * gain
    sigma = 1.0 / (1.0 + jnp.exp(-scaled))
    hidden = (scaled * sigma).astype(BF)
    hidden_p = mm(hidden, even_192[...]).astype(BF)

    for f in range(5):
        here = sc[1, f].reshape(96, 192)
        for s in range(2):
            moved = mm(cot[s], here) + mm(cot_rim[s, f], rim_c[s])
            sc[2 * s, f] = moved.astype(BF).reshape(6, 16, 192)

    def cot_view(a, i, j):
        return sc[2 - j, pl.ds(2 - a, 3), pl.ds(2 - i, 4)].reshape(192, 192)

    def planes(both, half, dst, at):
        dst[0, pl.ds(at, half)] = both[:half, :128]
        dst[1, pl.ds(at, half)] = jnp.concatenate([both[:half, 128:], both[half:, :64]], axis=1)
        dst[2, pl.ds(at, half)] = both[half:, 64:]

    def conv_taps(n, carry):
        a, i = n // 3, n % 3
        for j in range(3):
            at = pl.multiple_of((n * 3 + j) * 96, 96)
            planes(mm_tn(hidden_p, cot_view(a, i, j)), 96, fc, at)
        return carry

    lax.fori_loop(0, 9, conv_taps, 0)

    lane_row = lax.broadcasted_iota(jnp.int32, (8, 128), 0)

    def block_c(hh, i, t):
        at = (81 * (t * 8 + 4 * hh + i)) // 2
        spare = jnp.zeros((8, 128), F32)
        for q in range(3):
            spare = jnp.where(lane_row == q, fc[q, pl.ds(at + 40, 1)], spare)
        return jnp.concatenate([fc[q, pl.ds(at, 40)] for q in range(3)] + [spare], axis=0)

    def block_r(hh, i, t):
        at = 27 * (t * 8 + 4 * hh + i)
        return jnp.concatenate([fr[q, pl.ds(at, 32)] for q in range(3)], axis=0)

    parts = {
        0: (block_c, bs_c, br_c, xs_c, xr_c, ac_c, ys_c, yr_c),
        1: (block_r, bs_r, br_r, xs_r, xr_r, ac_r, ys_r, yr_r),
    }

    def core_copy(part, o):
        _, bs, br = parts[part][:3]
        i = (x + o) % 4
        return pltpu.make_async_remote_copy(
            src_ref=bs.at[i], dst_ref=br.at[i], send_sem=core_s.at[part * 4 + o],
            recv_sem=core_r.at[part * 4 + o], device_id=partner, device_id_type=MESH)

    def x_copy(part, o):
        xs, xr = parts[part][3:5]
        n = part * 3 + o - 1
        return pltpu.make_async_remote_copy(
            src_ref=xs.at[o - 1], dst_ref=xr.at[o - 1], send_sem=x_s.at[n],
            recv_sem=x_r.at[n], device_id=peer_x(o), device_id_type=MESH)

    def y_copy(part, o):
        ys, yr = parts[part][6:8]
        n = part * 7 + o - 1
        return pltpu.make_async_remote_copy(
            src_ref=ys.at[(y + o) % 8], dst_ref=yr.at[o - 1], send_sem=y_s.at[n],
            recv_sem=y_r.at[n], device_id=dev(o), device_id_type=MESH)

    def core_send(part):
        block, bs = parts[part][:2]
        for o in (1, 2, 3, 0):
            i = (x + o) % 4

            def fill(t, carry):
                bs[i, t] = block(1 - h, i, t).astype(BF)
                return carry

            lax.fori_loop(0, 8, fill, 0)
            core_copy(part, o).start()

    def x_send(part):
        block, _, br, xs, _, ac = parts[part][:6]
        for o in (1, 2, 3, 0):
            i = (x + o) % 4
            core_copy(part, o).wait()

            def fill(t, carry):
                total = block(h, i, t) + br[i, t].astype(F32)
                if o:
                    xs[o - 1, t] = total.astype(BF)
                else:
                    ac[t] = total
                return carry

            lax.fori_loop(0, 8, fill, 0)
            if o:
                x_copy(part, o).start()

    def y_send(part):
        xr, ac, ys = parts[part][4:7]
        for o in range(1, 4):
            x_copy(part, o).wait()

        def fill(t, carry):
            total = ac[t]
            for k in range(3):
                total += xr[k, t].astype(F32)
            ac[t] = total
            ys[t] = total.astype(BF)
            return carry

        lax.fori_loop(0, 8, fill, 0)
        for o in range(1, 8):
            y_copy(part, o).start()

    def y_sum(part):
        ac, _, yr = parts[part][5:8]
        for o in range(1, 8):
            y_copy(part, o).wait()
        total = ac[y]
        for k in range(7):
            total += yr[k].astype(F32)
        return total

    core_send(0)

    def back(n, total):
        a, i = n // 3, n % 3
        for j in range(3):
            total += mm_nt(cot_view(a, i, j), wc[a, i, j])
        return total

    hidden_grad = lax.fori_loop(0, 9, back, jnp.zeros((192, 192), F32))
    scaled_grad = hidden_grad * sigma * (1.0 + scaled * (1.0 - sigma))
    gain_local = jnp.sum(scaled_grad * normed, axis=0, keepdims=True)
    normed_grad = scaled_grad * gain
    delta = (
        inverse * (normed_grad - normed * jnp.mean(normed_grad * normed, axis=-1, keepdims=True))
    ).astype(BF)
    xd[:, 1:5] = delta.reshape(3, 4, 16, 192)
    rows_d = [
        remote(xd.at[f3, 1], xd.at[f3, 5], 11, dev(0, -1)),
        remote(xd.at[f3, 4], xd.at[f3, 0], 12, dev(0, 1)),
    ]
    for copy in rows_d:
        copy.start()

    tail = jnp.concatenate([gain_local[:, 128:], jnp.zeros((1, 64), F32)], axis=1)
    g_core[h] = jnp.where(lane_row == 0, gain_local[:, :128], jnp.where(lane_row == 1, tail, 0.0))

    def small(buf, at, ss, rs, n, to):
        return pltpu.make_async_remote_copy(
            src_ref=buf.at[at], dst_ref=buf.at[at], send_sem=ss.at[n], recv_sem=rs.at[n],
            device_id=to, device_id_type=MESH)

    g1 = small(g_core, h, gc_s, gc_r, 0, partner)
    g1.start()

    x_send(0)

    def lift_taps(n, carry):
        for j in range(3):
            at = pl.multiple_of((n * 3 + j) * 192, 192)
            view = slp[j, :, pl.ds(n, 4)].reshape(192, 384)
            planes(mm_tn(view, delta), 192, fr, at)
        return carry

    lax.fori_loop(0, 3, lift_taps, 0)
    core_send(1)

    for copy in rows_d:
        copy.wait()

    @pl.when(r == 0)
    def _():
        xd[:, 0] = jnp.zeros((3, 16, 192), BF)

    @pl.when(r == 7)
    def _():
        xd[:, 5] = jnp.zeros((3, 16, 192), BF)

    hs_d[...] = mm(edge_cot[:, :288], xd[...].reshape(288, 192)).astype(BF)
    cols_d = [
        remote(hs_d.at[pl.ds(0, 32)], rim_d.at[1], 13, dev(0, 0, -1)),
        remote(hs_d.at[pl.ds(32, 32)], rim_d.at[0], 14, dev(0, 0, 1)),
    ]
    for copy in cols_d:
        copy.start()

    g1.wait()
    g_x[x] = g_core[0] + g_core[1]
    g2 = [small(g_x, x, gx_s, gx_r, o - 1, peer_x(o)) for o in range(1, 4)]
    for copy in g2:
        copy.start()

    x_send(1)

    for copy in g2:
        copy.wait()
    g_y[y] = (g_x[0] + g_x[1]) + (g_x[2] + g_x[3])
    g3 = [small(g_y, y, gy_s, gy_r, o - 1, dev(o)) for o in range(1, 8)]
    for copy in g3:
        copy.start()

    y_send(0)

    for copy in cols_d:
        copy.wait()

    @pl.when(c == 0)
    def _():
        rim_d[0] = jnp.zeros((32, 192), BF)

    @pl.when(c == 7)
    def _():
        rim_d[1] = jnp.zeros((32, 192), BF)

    for t in range(3):
        here = xd[t].reshape(96, 192)
        for j in range(3):
            moved = mm(pair[j], here)
            if j != 1:
                moved += mm(pair_rim[j // 2, t], rim_d[j // 2])
            sd[j, t] = moved.astype(BF).reshape(6, 16, 192)

    def unlift(i, total):
        for j in range(3):
            total += mm_nt(sd[2 - j, :, pl.ds(2 - i, 4)].reshape(192, 192), wr[i, j])
        return total

    lifted_grad = lax.fori_loop(0, 3, unlift, jnp.zeros((192, 384), F32))
    gi_ref[...] = lifted_grad.reshape(3, 2, 4, 8, 384).sum(axis=2).astype(BF)

    y_send(1)

    for copy in g3:
        copy.wait()
    g_sum = g_y[0]
    for k in range(1, 8):
        g_sum += g_y[k]
    g_hi = g_sum.astype(BF).astype(F32)
    g_lo = g_sum - g_hi

    pw_c[...] = jnp.zeros((3, 48, 128), F32)
    sum_c = y_sum(0)
    for q in range(3):
        pw_c[q, 0:40] = sum_c[40 * q : 40 * q + 40]
        pw_c[q, 40:41] = sum_c[120 + q : 121 + q]
    pw_r[...] = y_sum(1).reshape(3, 32, 128)

    def fin_copy(q):
        to = (y, 4 * h + x, q)
        remote_one = pltpu.make_async_remote_copy(
            src_ref=ws.at[q], dst_ref=land.at[z], send_sem=fin_s.at[q], recv_sem=fin_r.at[z],
            device_id=to, device_id_type=MESH)
        own = jnp.logical_and(to[1] == r, q == c)
        return remote_one, own

    for q in range(8):
        low = (27 * q) // 8
        for k in range(3):
            right = pw_r[k, low : low + 8]
            if k < 2:
                extra = (g_hi, g_lo)[k]
                right = jnp.where(lane_row == 5, extra[0:1], jnp.where(lane_row == 6, extra[1:2], right))
            both = jnp.concatenate([pw_c[k, 5 * q : 5 * q + 8], right], axis=0)
            ws[q, 16 * k : 16 * k + 16] = both.astype(BF)
        remote_one, own = fin_copy(q)

        @pl.when(jnp.logical_not(own))
        def _():
            remote_one.start()

        @pl.when(own)
        def _():
            pltpu.make_async_copy(ws.at[q], land.at[z], fin_r.at[z]).start()

    for q in range(8):
        remote_one, own = fin_copy(q)

        @pl.when(jnp.logical_not(own))
        def _():
            remote_one.wait_send()

    total = jnp.zeros((48, 128), F32)
    for k in range(8):
        pltpu.make_async_copy(ws.at[0], land.at[k], fin_r.at[k]).wait()
        total += land[k].astype(F32)

    og_ref[...] = jnp.where(
        lane_row == 0, total[13:14] + total[29:30], jnp.where(lane_row == 1, total[14:15] + total[30:31], 0.0)
    )
    flat_c[...] = jnp.zeros((24, 128), F32)
    flat_r[...] = jnp.zeros((24, 128), F32)
    for k in range(3):
        for u in range(6):
            flat_c[3 * u + k : 3 * u + k + 1] = total[16 * k + u : 16 * k + u + 1]
        for u in range(5):
            flat_r[3 * u + k : 3 * u + k + 1] = total[16 * k + 8 + u : 16 * k + 9 + u]

    def cut(flat, off):
        lane = lax.broadcasted_iota(jnp.int32, (16, 128), 1)
        m, s = off // 128, off % 128
        turn = (128 - s) % 128
        one = pltpu.roll(flat[pl.ds(m, 16)], turn, 1)
        two = pltpu.roll(flat[pl.ds(m + 1, 16)], turn, 1)
        return jnp.where(lane < 128 - s, one, two)

    oc_ref[...] = cut(flat_c, 192 * (r % 2) + 24 * c)
    or_ref[...] = cut(flat_r, 1296 * c - 384 * ((27 * c) // 8))


def local(latent, cotangent, resample_weight, conv_weight, norm_gain):
    vm, hbm = pl.BlockSpec(memory_space=pltpu.VMEM), pl.BlockSpec(memory_space=pl.ANY)
    consts = selectors()
    dma, V = pltpu.SemaphoreType.DMA, pltpu.VMEM
    c, s = 128, 96

    def reduce_buffers(n):
        return [
            V((4, 8, n, 128), BF), V((4, 8, n, 128), BF), V((3, 8, n, 128), BF), V((3, 8, n, 128), BF),
            V((8, n, 128), F32), V((8, n, 128), BF), V((7, n, 128), BF),
        ]

    scratch = [
        V((3, 3, 384, 192), BF), V((3, 3, 3, 192, 192), BF),
        V((3, 5, 6, 16, 192), BF), V((3, 4, 16, 384), BF), V((3, 4, 16, 384), BF),
        V((64, 192), BF), V((32, 384), BF), V((64, 192), BF),
        V((2, 32, 192), BF), V((2, 16, 384), BF), V((2, 32, 192), BF),
        V((3, 3, 6, 16, 384), BF), V((3, 3, 6, 16, 384), BF),
        V((3, 6, 16, 192), BF), V((3, 3, 6, 16, 192), BF),
        V((3, 2592 + 48, 128), F32), V((3, 1728 + 32, 128), F32),
        *reduce_buffers(c), *reduce_buffers(s),
        V((2, 8, 128), F32), V((4, 8, 128), F32), V((8, 8, 128), F32),
        V((3, 48, 128), F32), V((3, 32, 128), F32),
        V((8, 48, 128), BF), V((8, 48, 128), BF), V((24, 128), F32), V((24, 128), F32),
        dma((2,)), dma((15,)), dma((15,)), dma((8,)), dma((8,)), dma((6,)), dma((6,)), dma((14,)), dma((14,)),
        dma((8,)), dma((8,)), dma((1,)), dma((1,)), dma((3,)), dma((3,)), dma((7,)), dma((7,)),
    ]
    gi, oc, orr, og = pl.pallas_call(
        kernel,
        out_shape=[
            jax.ShapeDtypeStruct((3, 2, 8, 384), BF),
            jax.ShapeDtypeStruct((16, 128), F32),
            jax.ShapeDtypeStruct((16, 128), F32),
            jax.ShapeDtypeStruct((8, 128), F32),
        ],
        in_specs=[vm, vm, vm, hbm, hbm] + [vm] * len(consts),
        out_specs=[vm] * 4,
        scratch_shapes=scratch,
        compiler_params=pltpu.CompilerParams(
            collective_id=0, has_side_effects=True, vmem_limit_bytes=56 * 2**20
        ),
        cost_estimate=pl.CostEstimate(flops=1_600_000_000, bytes_accessed=5_000_000, transcendentals=40_000),
    )(latent, cotangent, norm_gain.reshape(1, 192), resample_weight, conv_weight, *consts)
    return gi, orr.reshape(-1)[:1296], oc.reshape(-1)[:1944], og.reshape(-1)[:192]


def solution(mesh):
    in_specs = (P("tm", "rows", "cols", None), P("tm", "rows", "cols", None), P(), P(), P())
    out_specs = (
        P("tm", "rows", "cols", None),
        P(("tm", "rows", "cols")),
        P(("tm", "rows", "cols")),
        P(),
    )
    return jax.shard_map(local, mesh=mesh, in_specs=in_specs, out_specs=out_specs, check_vma=False)
```

```python
import functools

import jax
import jax.numpy as jnp
import numpy as np
from jax import lax
from jax.experimental import pallas as pl
from jax.experimental.pallas import tpu as pltpu
from jax.sharding import PartitionSpec as P

EPSILON = 1e-06
MESH = pl.DeviceIdType.MESH
BF = jnp.bfloat16
F32 = jnp.float32


def selectors():
    low = [0, 1, 1, 2, 2, 3]

    def zeros(*dims):
        return np.zeros(dims, np.float32)

    widen = zeros(96, 48)
    for t in range(3):
        for l in range(2):
            for c in range(16):
                widen[t * 32 + l * 16 + c, t * 16 + l * 8 + c // 2] = 1
    even_192, even_384 = zeros(192, 192), zeros(384, 384)
    for u in range(96):
        even_192[u, 2 * u] = even_192[96 + u, 2 * u + 1] = 1
    for u in range(192):
        even_384[2 * u, u] = even_384[2 * u + 1, 192 + u] = 1
    lift, lift_rim = zeros(3, 96, 64), zeros(2, 3, 96, 48)
    cot, cot_rim = zeros(2, 96, 96), zeros(2, 5, 96, 96)
    pair, pair_rim = zeros(3, 96, 96), zeros(2, 3, 96, 32)

    def slot(at, last, frame, late):
        kind = 1 if at == 0 else 2 if at == last else 0
        row = frame if kind else frame * (last - 1) + at - 1
        return (kind + 3 * late) * 16 + row

    for row in range(6):
        for c in range(16):
            out = row * 16 + c
            par = row * 16 + (c % 2) * 8 + c // 2
            for j in range(3):
                at = c + j - 1
                if 0 <= at < 16:
                    lift[j, out, low[row] * 16 + at] = 1
                    pair[j, par, row * 16 + at] = 1
                    if j != 1:
                        cot[j // 2, out, row * 16 + at] = 1
                else:
                    side = j // 2
                    for f in range(5):
                        cot_rim[side, f, out, slot(row, 5, f % 3, f // 3)] = 1
                    for f in range(3):
                        lift_rim[side, f, out, slot(low[row], 3, f, 0)] = 1
                        pair_rim[side, f, par, f * 6 + row] = 1
    edge_cot, edge_low, edge_delta = zeros(96, 192), zeros(96, 96), zeros(64, 288)
    for side, col in ((0, 0), (1, 15)):
        for n in range(18):
            edge_delta[side * 32 + n, n * 16 + col] = 1
        for t in range(3):
            for rows, edge in ((4, edge_cot), (2, edge_low)):
                for row in range(rows):
                    edge[side * 48 + t * rows + row, (t * rows + row) * 16 + col] = 1
                edge[side * 48 + 16 + t, t * rows * 16 + col] = 1
                edge[side * 48 + 32 + t, (t * rows + rows - 1) * 16 + col] = 1
    parts = (widen, even_192, even_384, lift, lift_rim, cot, cot_rim, pair, pair_rim, edge_cot, edge_low, edge_delta)
    return [jnp.asarray(p, BF) for p in parts]


def mm(a, b):
    return jnp.dot(a, b, preferred_element_type=F32)


def mm_nt(a, b):
    return lax.dot_general(a, b, (((1,), (1,)), ((), ())), preferred_element_type=F32)


def mm_tn(a, b):
    return lax.dot_general(a, b, (((0,), (0,)), ((), ())), preferred_element_type=F32)


def kernel(*refs):
    (latent_hbm, cot_hbm, gain_hbm, wr_hbm, wc_hbm), refs = refs[:5], refs[5:]
    const_hbm, (gi_ref, oc_ref, or_ref, og_ref), refs = refs[:12], refs[12:16], refs[16:]
    consts, refs = refs[:12], refs[12:]
    (widen, even_192, even_384, lift, lift_rim, cot, cot_rim, pair, pair_rim, edge_cot, edge_low, edge_delta) = consts
    (
        latv, gain_v, wr, wc, sc, lc, lcp, hs, rim, hs_d, rim_d, sl, slp, xd, sd, fc, fr,
        g_core, g_x, g_y, sum_c, pw_c, pw_r, ws_c, ws_r, land_c, land_r, pack, flat_c, flat_r,
        load_sem, ssem, rsem, core_s, core_r, x_s, x_r, y_s, y_r, fin_s, fin_r,
        gc_s, gc_r, gx_s, gx_r, gy_s, gy_r,
    ), refs = refs[:47], refs[47:]
    bufs = [refs[5 * p : 5 * p + 5] for p in range(3)]
    yr_c, yr_r = refs[18:20]
    y_bufs = [(refs[15], yr_c), (refs[16], yr_c), (refs[17], yr_r)]

    y, r, c = lax.axis_index("tm"), lax.axis_index("rows"), lax.axis_index("cols")
    h, zl = r % 2, r // 2
    x, zh = c % 4, c // 4
    z = zh * 4 + zl

    def dev(dy=0, dr=0, dc=0):
        return ((y + dy + 8) % 8, (r + dr + 8) % 8, (c + dc + 8) % 8)

    partner = (y, zl * 2 + 1 - h, c)

    def peer_x(o):
        return (y, r, zh * 4 + (x + o) % 4)

    bar = pltpu.get_barrier_semaphore()
    sources = [dev(dy, dr, dc) for dc in (1, -1, 0) for dr in (-1, 0, 1) for dy in (0, 1) if (dy, dr, dc) != (0, 0, 0)]
    sources += [partner] + [peer_x(o) for o in range(1, 4)] + [dev(o) for o in range(1, 8)]
    for d in sources:
        pl.semaphore_signal(bar, inc=1, device_id=d, device_id_type=MESH)
    for q in range(8):
        src = (y, 2 * (q % 4) + r // 4, (q // 4) * 4 + r % 4)

        @pl.when(jnp.logical_or(src[1] != r, src[2] != c))
        def _():
            pl.semaphore_signal(bar, inc=1, device_id=src, device_id_type=MESH)

    mine = jnp.where(r == 4 * h + x, 1, 0)

    f3, f2, late = pl.ds(0, 3), pl.ds(0, 2), pl.ds(3, 2)
    targets = [(latent_hbm, latv), (cot_hbm, sc.at[1, f3, pl.ds(1, 4)]), (gain_hbm, gain_v)]
    targets += [(a, b) for a, b in zip(const_hbm, consts)] + [(wr_hbm, wr), (wc_hbm, wc)]
    loads = [pltpu.make_async_copy(a, b, load_sem.at[n]) for n, (a, b) in enumerate(targets)]
    for copy in loads:
        copy.start()
    for copy in loads[:-2]:
        copy.wait()

    own_low = latv[...].astype(F32).reshape(48, 384).astype(BF)
    own_low = mm(widen[...], own_low).astype(BF)
    lc[:, 1:3] = own_low.reshape(3, 2, 16, 384)
    hs[:, :, :, 0:384] = mm(edge_low[...], own_low).astype(BF).reshape(2, 3, 16, 384)
    own_cot = sc[1, 0:3, 1:5].reshape(192, 192)
    hs[:, :, :, 384:576] = mm(edge_cot[...], own_cot).astype(BF).reshape(2, 3, 16, 192)

    pl.semaphore_wait(bar, len(sources) + 8 - mine)

    def remote(src, dst, n, to):
        return pltpu.make_async_remote_copy(
            src_ref=src, dst_ref=dst, send_sem=ssem.at[n], recv_sem=rsem.at[n],
            device_id=to, device_id_type=MESH,
        )

    halo = []
    for s, dc in ((0, -1), (1, 1)):
        for n, (tile, dy, dr) in enumerate(((0, 0, 0), (2, 0, 1), (1, 0, -1), (0, -1, 0), (2, -1, 1), (1, -1, -1))):
            halo.append(remote(hs.at[s, tile], rim.at[1 - s, n], 11 + 6 * s + n, dev(dy, dr, dc)))
    halo += [
        remote(lc.at[f3, 1], lc.at[f3, 3], 5, dev(0, -1)),
        remote(lc.at[f3, 2], lc.at[f3, 0], 6, dev(0, 1)),
        remote(sc.at[1, f3, 1], sc.at[1, f3, 5], 0, dev(0, -1)),
        remote(sc.at[1, f3, 4], sc.at[1, f3, 0], 1, dev(0, 1)),
        remote(sc.at[1, f2, pl.ds(1, 4)], sc.at[1, late, pl.ds(1, 4)], 2, dev(-1, 0)),
        remote(sc.at[1, f2, 1], sc.at[1, late, 5], 3, dev(-1, -1)),
        remote(sc.at[1, f2, 4], sc.at[1, late, 0], 4, dev(-1, 1)),
    ]
    for copy in halo:
        copy.start()
    for copy in loads[-2:]:
        copy.wait()
    for copy in halo:
        copy.wait()

    @pl.when(r == 0)
    def _():
        sc[1, :, 0] = jnp.zeros((5, 16, 192), BF)
        lc[:, 0] = jnp.zeros((3, 16, 384), BF)
        for n in (1, 4):
            rim[:, n] = jnp.zeros((2, 16, 576), BF)

    @pl.when(r == 7)
    def _():
        sc[1, :, 5] = jnp.zeros((5, 16, 192), BF)
        lc[:, 3] = jnp.zeros((3, 16, 384), BF)
        for n in (2, 5):
            rim[:, n] = jnp.zeros((2, 16, 576), BF)

    @pl.when(y == 7)
    def _():
        sc[1, 3:5] = jnp.zeros((2, 6, 16, 192), BF)
        rim[:, 3:6] = jnp.zeros((2, 3, 16, 576), BF)

    @pl.when(c == 0)
    def _():
        rim[0] = jnp.zeros((6, 16, 576), BF)

    @pl.when(c == 7)
    def _():
        rim[1] = jnp.zeros((6, 16, 576), BF)

    lcp[...] = mm(lc[...].reshape(192, 384), even_384[...]).astype(BF).reshape(3, 4, 16, 384)
    rim_l = [rim[s, 0:3, :, 0:384].reshape(48, 384) for s in range(2)]
    rim_p = [mm(rim_l[s], even_384[...]).astype(BF) for s in range(2)]
    for t in range(3):
        here = lc[t].reshape(64, 384)
        here_p = lcp[t].reshape(64, 384)
        for j in range(3):
            wide, wide_p = mm(lift[j], here), mm(lift[j], here_p)
            if j != 1:
                wide += mm(lift_rim[j // 2, t], rim_l[j // 2])
                wide_p += mm(lift_rim[j // 2, t], rim_p[j // 2])
            sl[j, t] = wide.astype(BF).reshape(6, 16, 384)
            slp[j, t] = wide_p.astype(BF).reshape(6, 16, 384)

    def fwd(i, total):
        for j in range(3):
            total += mm_nt(sl[j, :, pl.ds(i, 4)].reshape(192, 384), wr[i, j])
        return total

    z_float = lax.fori_loop(0, 3, fwd, jnp.zeros((192, 192), F32)).astype(BF).astype(F32)
    gain = gain_v[...]
    inverse = lax.rsqrt(jnp.mean(z_float * z_float, axis=-1, keepdims=True) + EPSILON)
    normed = z_float * inverse
    scaled = normed * gain
    sigma = 1.0 / (1.0 + jnp.exp(-scaled))
    hidden = (scaled * sigma).astype(BF)
    hidden_t = mm_nt(even_192[...], hidden).astype(BF)

    for f in range(5):
        here = sc[1, f].reshape(96, 192)
        for s in range(2):
            moved = mm(cot[s], here) + mm(cot_rim[s, f], rim[s, :, :, 384:576].reshape(96, 192))
            sc[2 * s, f] = moved.astype(BF).reshape(6, 16, 192)

    def cot_view(a, i, j):
        return sc[2 - j, pl.ds(2 - a, 3), pl.ds(2 - i, 4)].reshape(192, 192)

    def planes(both, half, dst, at):
        dst[0, pl.ds(at, half)] = both[:half, :128]
        dst[1, pl.ds(at, half)] = jnp.concatenate([both[:half, 128:], both[half:, :64]], axis=1)
        dst[2, pl.ds(at, half)] = both[half:, 64:]

    def conv_taps(n, carry):
        a, i = n // 3, n % 3
        for j in range(3):
            at = pl.multiple_of((n * 3 + j) * 96, 96)
            planes(mm(hidden_t, cot_view(a, i, j)), 96, fc, at)
        return carry

    lane_row = lax.broadcasted_iota(jnp.int32, (8, 128), 0)

    def block_c(hh, i, t):
        at = (81 * (t * 8 + 4 * hh + i)) // 2
        spare = jnp.zeros((8, 128), F32)
        for q in range(3):
            spare = jnp.where(lane_row == q, fc[q, pl.ds(at + 40, 1)], spare)
        return jnp.concatenate([fc[q, pl.ds(at, 40)] for q in range(3)] + [spare], axis=0)

    def block_r(hh, i, t):
        at = 27 * (t * 8 + 4 * hh + i)
        return jnp.concatenate([fr[q, pl.ds(at, 32)] for q in range(3)], axis=0)

    parts = [(block_c, 0, 4), (block_c, 4, 8), (block_r, 0, 8)]

    def core_copy(p, o):
        bs, br = bufs[p][:2]
        i = (x + o) % 4
        return pltpu.make_async_remote_copy(
            src_ref=bs.at[i], dst_ref=br.at[i], send_sem=core_s.at[p * 4 + o],
            recv_sem=core_r.at[p * 4 + o], device_id=partner, device_id_type=MESH)

    def x_copy(p, m):
        xs, xr = bufs[p][2:4]
        return pltpu.make_async_remote_copy(
            src_ref=xs.at[m], dst_ref=xr.at[m], send_sem=x_s.at[p * 6 + m],
            recv_sem=x_r.at[p * 6 + m], device_id=peer_x(1 if m % 2 == 0 else 3), device_id_type=MESH)

    def core_send(p):
        block, lo, hi = parts[p]
        bs = bufs[p][0]
        for o in (2, 1, 3, 0):
            i = (x + o) % 4

            def fill(t, carry):
                bs[i, t - lo] = block(1 - h, i, t).astype(BF)
                return carry

            lax.fori_loop(lo, hi, fill, 0)
            core_copy(p, o).start()

    def x_fill(p, m, i, first, last, relayed):
        block, lo, _ = parts[p]
        _, br, xs, xr = bufs[p][:4]

        def fill(t, carry):
            total = block(h, i, t) + br[i, t - lo].astype(F32)
            if relayed:
                total += xr[m - 4, t - first].astype(F32)
            xs[m, t - first] = total.astype(BF)
            return carry

        lax.fori_loop(first, last, fill, 0)
        x_copy(p, m).start()

    def x_first(p):
        block, lo, hi = parts[p]
        mid = (lo + hi) // 2
        br, ac = bufs[p][1], bufs[p][4]
        core_copy(p, 2).wait()
        x_fill(p, 0, (x + 2) % 4, lo, mid, False)
        x_fill(p, 1, (x + 2) % 4, mid, hi, False)
        core_copy(p, 1).wait()
        x_fill(p, 2, (x + 1) % 4, mid, hi, False)
        core_copy(p, 3).wait()
        x_fill(p, 3, (x + 3) % 4, lo, mid, False)
        core_copy(p, 0).wait()

        def keep(t, carry):
            ac[t - lo] = block(h, x, t) + br[x, t - lo].astype(F32)
            return carry

        lax.fori_loop(lo, hi, keep, 0)

    def x_second(p):
        _, lo, hi = parts[p]
        mid = (lo + hi) // 2
        x_copy(p, 0).wait()
        x_fill(p, 4, (x + 1) % 4, lo, mid, True)
        x_copy(p, 1).wait()
        x_fill(p, 5, (x + 3) % 4, mid, hi, True)

    def y_copy(p, t):
        ys, yr = y_bufs[p]
        n = (0, 4, 8)[p] + t - parts[p][1]
        return pltpu.make_async_remote_copy(
            src_ref=ys.at[t - parts[p][1]], dst_ref=yr.at[y], send_sem=y_s.at[n],
            recv_sem=y_r.at[min(p, 2) // 2 * 8 + y], device_id=(t, r, c), device_id_type=MESH)

    def y_send(p):
        _, lo, hi = parts[p]
        mid = (lo + hi) // 2
        xr, ac = bufs[p][3], bufs[p][4]
        ys = y_bufs[p][0]
        for m in range(2, 6):
            x_copy(p, m).wait()
        for first, last, one, two in ((lo, mid, 4, 3), (mid, hi, 5, 2)):

            def fill(t, carry):
                total = ac[t - lo] + xr[one, t - first].astype(F32) + xr[two, t - first].astype(F32)
                ac[t - lo] = total
                ys[t - lo] = total.astype(BF)
                return carry

            lax.fori_loop(first, last, fill, 0)
        for t in range(lo, hi):

            @pl.when(y != t)
            def _():
                y_copy(p, t).start()

    def y_wait_send(p):
        _, lo, hi = parts[p]
        for t in range(lo, hi):

            @pl.when(y != t)
            def _():
                y_copy(p, t).wait_send()

    def y_sum(p):
        _, lo, _ = parts[p]
        ac, yr = bufs[p][4], y_bufs[p][1]
        total = ac[y - lo]
        for o in range(1, 8):
            k = (y + o) % 8
            pltpu.make_async_copy(yr.at[k], yr.at[k], y_r.at[min(p, 2) // 2 * 8 + k]).wait()
            total += yr[k].astype(F32)
        return total

    lax.fori_loop(0, 5, conv_taps, 0)
    core_send(0)
    lax.fori_loop(5, 7, conv_taps, 0)
    x_first(0)
    lax.fori_loop(7, 9, conv_taps, 0)
    core_send(1)

    def back(n, total):
        a, i = n // 3, n % 3
        for j in range(3):
            total += mm_nt(cot_view(a, i, j), wc[a, i, j])
        return total

    hidden_grad = lax.fori_loop(0, 9, back, jnp.zeros((192, 192), F32))
    x_first(1)
    x_second(0)
    scaled_grad = hidden_grad * sigma * (1.0 + scaled * (1.0 - sigma))
    gain_local = jnp.sum(scaled_grad * normed, axis=0, keepdims=True)
    normed_grad = scaled_grad * gain
    delta = (
        inverse * (normed_grad - normed * jnp.mean(normed_grad * normed, axis=-1, keepdims=True))
    ).astype(BF)
    xd[:, 1:5] = delta.reshape(3, 4, 16, 192)
    rows_d = [
        remote(xd.at[f3, 1], xd.at[f3, 5], 7, dev(0, -1)),
        remote(xd.at[f3, 4], xd.at[f3, 0], 8, dev(0, 1)),
    ]
    for copy in rows_d:
        copy.start()

    tail = jnp.concatenate([gain_local[:, 128:], jnp.zeros((1, 64), F32)], axis=1)
    g_core[h] = jnp.where(lane_row == 0, gain_local[:, :128], jnp.where(lane_row == 1, tail, 0.0))

    def small(buf, at, ss, rs, n, to):
        return pltpu.make_async_remote_copy(
            src_ref=buf.at[at], dst_ref=buf.at[at], send_sem=ss.at[n], recv_sem=rs.at[n],
            device_id=to, device_id_type=MESH)

    g1 = small(g_core, h, gc_s, gc_r, 0, partner)
    g1.start()


    def lift_taps(n, carry):
        for j in range(3):
            at = pl.multiple_of((n * 3 + j) * 192, 192)
            view = slp[j, :, pl.ds(n, 4)].reshape(192, 384)
            planes(mm_tn(view, delta), 192, fr, at)
        return carry

    lax.fori_loop(0, 3, lift_taps, 0)
    core_send(2)
    x_second(1)
    x_first(2)

    for copy in rows_d:
        copy.wait()

    @pl.when(r == 0)
    def _():
        xd[:, 0] = jnp.zeros((3, 16, 192), BF)

    @pl.when(r == 7)
    def _():
        xd[:, 5] = jnp.zeros((3, 16, 192), BF)

    hs_d[...] = mm(edge_delta[...], xd[...].reshape(288, 192)).astype(BF)
    cols_d = [
        remote(hs_d.at[pl.ds(0, 32)], rim_d.at[1], 9, dev(0, 0, -1)),
        remote(hs_d.at[pl.ds(32, 32)], rim_d.at[0], 10, dev(0, 0, 1)),
    ]
    for copy in cols_d:
        copy.start()

    g1.wait()
    g_x[x] = g_core[0] + g_core[1]
    g2 = [small(g_x, x, gx_s, gx_r, o - 1, peer_x(o)) for o in range(1, 4)]
    for copy in g2:
        copy.start()

    y_send(0)
    x_second(2)

    for copy in g2:
        copy.wait()
    g_y[y] = (g_x[0] + g_x[1]) + (g_x[2] + g_x[3])
    g3 = [small(g_y, y, gy_s, gy_r, o - 1, dev(o)) for o in range(1, 8)]
    for copy in g3:
        copy.start()

    y_send(1)

    for copy in cols_d:
        copy.wait()

    @pl.when(c == 0)
    def _():
        rim_d[0] = jnp.zeros((32, 192), BF)

    @pl.when(c == 7)
    def _():
        rim_d[1] = jnp.zeros((32, 192), BF)

    for t in range(3):
        here = xd[t].reshape(96, 192)
        for j in range(3):
            moved = mm(pair[j], here)
            if j != 1:
                moved += mm(pair_rim[j // 2, t], rim_d[j // 2])
            sd[j, t] = moved.astype(BF).reshape(6, 16, 192)

    def unlift(i, total):
        for j in range(3):
            total += mm(sd[2 - j, :, pl.ds(2 - i, 4)].reshape(192, 192), wr[i, j])
        return total

    lifted_grad = lax.fori_loop(0, 3, unlift, jnp.zeros((192, 384), F32))
    gi_ref[...] = lifted_grad.reshape(3, 2, 4, 8, 384).sum(axis=2).astype(BF)

    y_send(2)

    for copy in g3:
        copy.wait()
    g_sum = g_y[0]
    for k in range(1, 8):
        g_sum += g_y[k]
    g_hi = g_sum.astype(BF).astype(F32)
    g_lo = g_sum - g_hi

    extra = jnp.concatenate([g_hi[0:2], g_lo[0:2], jnp.zeros((4, 128), F32)], axis=0)

    def fin_copy(n, q):
        to = (y, 4 * h + x, q)
        src, dst = ((ws_c, land_c), (ws_r, land_r))[n]
        remote_one = pltpu.make_async_remote_copy(
            src_ref=src.at[q], dst_ref=dst.at[z], send_sem=fin_s.at[n * 8 + q], recv_sem=fin_r.at[n * 8 + z],
            device_id=to, device_id_type=MESH)
        return remote_one, jnp.logical_and(to[1] == r, q == c)

    def fin_start(n, q):
        remote_one, own = fin_copy(n, q)
        src, dst = ((ws_c, land_c), (ws_r, land_r))[n]

        @pl.when(jnp.logical_not(own))
        def _():
            remote_one.start()

        @pl.when(own)
        def _():
            pltpu.make_async_copy(src.at[q], dst.at[z], fin_r.at[n * 8 + z]).start()

    @pl.when(y < 4)
    def _():
        sum_c[...] = y_sum(0)

    @pl.when(y >= 4)
    def _():
        sum_c[...] = y_sum(1)

    pw_c[...] = jnp.zeros((3, 48, 128), F32)
    for q in range(3):
        pw_c[q, 0:40] = sum_c[40 * q : 40 * q + 40]
        pw_c[q, 40:41] = sum_c[120 + q : 121 + q]
    for q in range(8):
        rows = [pw_c[k, 5 * q : 5 * q + 8] for k in range(3)]
        ws_c[q] = jnp.concatenate(rows + [extra], axis=0).astype(BF)
        fin_start(0, q)

    pw_r[...] = y_sum(2).reshape(3, 32, 128)
    pack[...] = jnp.zeros((16, 128), F32)
    for q in range(8):
        low = (27 * q) // 8
        for k in range(3):
            pack[5 * k : 5 * k + 5] = pw_r[k, low : low + 5]
        ws_r[q] = pack[...].astype(BF)
        fin_start(1, q)

    def fin_sum(n):
        src, dst = ((ws_c, land_c), (ws_r, land_r))[n]
        total = jnp.zeros(dst.shape[1:], F32)
        for k in range(8):
            pltpu.make_async_copy(src.at[0], dst.at[k], fin_r.at[n * 8 + k]).wait()
            total += dst[k].astype(F32)
        return total

    flat_c[...] = jnp.zeros((24, 128), F32)
    flat_r[...] = jnp.zeros((24, 128), F32)
    total = fin_sum(0)
    og_ref[...] = total[24:26] + total[26:28]
    for k in range(3):
        for u in range(6):
            flat_c[3 * u + k : 3 * u + k + 1] = total[8 * k + u : 8 * k + u + 1]

    def cut(flat, off):
        lane = lax.broadcasted_iota(jnp.int32, (16, 128), 1)
        m, s = off // 128, off % 128
        turn = (128 - s) % 128
        one = pltpu.roll(flat[pl.ds(m, 16)], turn, 1)
        two = pltpu.roll(flat[pl.ds(m + 1, 16)], turn, 1)
        return jnp.where(lane < 128 - s, one, two)

    oc_ref[...] = cut(flat_c, 192 * (r % 2) + 24 * c)

    for p in range(3):
        y_wait_send(p)
    for n in range(2):
        for q in range(8):
            remote_one, own = fin_copy(n, q)

            @pl.when(jnp.logical_not(own))
            def _():
                remote_one.wait_send()

    total = fin_sum(1)
    for k in range(3):
        for u in range(5):
            flat_r[3 * u + k : 3 * u + k + 1] = total[5 * k + u : 5 * k + u + 1]
    or_ref[...] = cut(flat_r, 1296 * c - 384 * ((27 * c) // 8))


def hand_over(gi, oc, orr, og, gi_out, oc_out, or_out, og_out, sem):
    pairs = ((gi, gi_out), (oc, oc_out), (orr, or_out), (og, og_out))
    copies = [pltpu.make_async_copy(a, b, sem.at[n]) for n, (a, b) in enumerate(pairs)]
    for copy in copies:
        copy.start()
    for copy in copies:
        copy.wait()


def local(latent, cotangent, resample_weight, conv_weight, norm_gain):
    vm = pl.BlockSpec(memory_space=pltpu.VMEM)
    far = pl.BlockSpec(memory_space=pltpu.HBM)
    consts = selectors()
    dma, V = pltpu.SemaphoreType.DMA, pltpu.VMEM

    def reduce_buffers(n, tms):
        return [
            V((4, tms, n, 128), BF), V((4, tms, n, 128), BF), V((6, tms // 2, n, 128), BF),
            V((6, tms // 2, n, 128), BF), V((tms, n, 128), F32),
        ]

    scratch = [V(a.shape, BF) for a in consts]
    scratch += [
        V((3, 2, 8, 384), BF), V((1, 192), F32), V((3, 3, 192, 384), BF), V((3, 3, 3, 192, 192), BF),
        V((3, 5, 6, 16, 192), BF), V((3, 4, 16, 384), BF), V((3, 4, 16, 384), BF),
        V((2, 3, 16, 576), BF), V((2, 6, 16, 576), BF), V((64, 192), BF), V((2, 32, 192), BF),
        V((3, 3, 6, 16, 384), BF), V((3, 3, 6, 16, 384), BF),
        V((3, 6, 16, 192), BF), V((3, 3, 6, 16, 192), BF),
        V((3, 2592 + 48, 128), F32), V((3, 1728 + 32, 128), F32),
        V((2, 8, 128), F32), V((4, 8, 128), F32), V((8, 8, 128), F32),
        V((128, 128), F32), V((3, 48, 128), F32), V((3, 32, 128), F32),
        V((8, 32, 128), BF), V((8, 16, 128), BF), V((8, 32, 128), BF), V((8, 16, 128), BF),
        V((16, 128), F32), V((24, 128), F32), V((24, 128), F32),
        dma((17,)), dma((23,)), dma((23,)), dma((12,)), dma((12,)), dma((18,)), dma((18,)), dma((16,)), dma((16,)),
        dma((16,)), dma((16,)), dma((1,)), dma((1,)), dma((3,)), dma((3,)), dma((7,)), dma((7,)),
        *reduce_buffers(128, 4), *reduce_buffers(128, 4), *reduce_buffers(96, 8),
        V((4, 128, 128), BF), V((4, 128, 128), BF), V((8, 96, 128), BF), V((8, 128, 128), BF), V((8, 96, 128), BF),
    ]
    gi, oc, orr, og = pl.pallas_call(
        kernel,
        out_shape=[
            jax.ShapeDtypeStruct((3, 2, 8, 384), BF),
            jax.ShapeDtypeStruct((16, 128), F32),
            jax.ShapeDtypeStruct((16, 128), F32),
            jax.ShapeDtypeStruct((2, 128), F32),
        ],
        in_specs=[far] * (5 + len(consts)),
        out_specs=[vm] * 4,
        scratch_shapes=scratch,
        compiler_params=pltpu.CompilerParams(
            collective_id=0, has_side_effects=True, vmem_limit_bytes=56 * 2**20
        ),
        cost_estimate=pl.CostEstimate(flops=1_600_000_000, bytes_accessed=5_000_000, transcendentals=40_000),
    )(latent, cotangent, norm_gain.reshape(1, 192), jnp.swapaxes(resample_weight, 2, 3), conv_weight, *consts)
    shapes = [jax.ShapeDtypeStruct(a.shape, a.dtype) for a in (gi, oc, orr, og)]
    gi, oc, orr, og = pl.pallas_call(
        hand_over, out_shape=shapes, in_specs=[far] * 4, out_specs=[far] * 4, scratch_shapes=[dma((4,))]
    )(gi, oc, orr, og)
    return gi, orr.reshape(-1)[:1296], oc.reshape(-1)[:1944], og.reshape(-1)[:192]


def solution(mesh):
    in_specs = (P("tm", "rows", "cols", None), P("tm", "rows", "cols", None), P(), P(), P())
    out_specs = (
        P("tm", "rows", "cols", None),
        P(("tm", "rows", "cols")),
        P(("tm", "rows", "cols")),
        P(),
    )
    return jax.shard_map(local, mesh=mesh, in_specs=in_specs, out_specs=out_specs, check_vma=False)
```

```python
import functools

import jax
import jax.numpy as jnp
import numpy as np
from jax import lax
from jax.experimental import pallas as pl
from jax.experimental.pallas import tpu as pltpu
from jax.sharding import PartitionSpec as P

EPSILON = 1e-06
MESH = pl.DeviceIdType.MESH
BF = jnp.bfloat16
F32 = jnp.float32


def selectors():
    low = [0, 1, 1, 2, 2, 3]

    def zeros(*dims):
        return np.zeros(dims, np.float32)

    widen = zeros(96, 48)
    for t in range(3):
        for l in range(2):
            for c in range(16):
                widen[t * 32 + l * 16 + c, t * 16 + l * 8 + c // 2] = 1
    even_192, even_384 = zeros(192, 192), zeros(384, 384)
    for u in range(96):
        even_192[u, 2 * u] = even_192[96 + u, 2 * u + 1] = 1
    for u in range(192):
        even_384[2 * u, u] = even_384[2 * u + 1, 192 + u] = 1
    lift, lift_rim = zeros(3, 96, 64), zeros(2, 3, 96, 16)
    cot, cot_rim = zeros(2, 96, 96), zeros(2, 5, 96, 32)
    pair, pair_rim = zeros(3, 96, 96), zeros(2, 3, 96, 32)

    for row in range(6):
        for c in range(16):
            out = row * 16 + c
            par = row * 16 + (c % 2) * 8 + c // 2
            for j in range(3):
                at = c + j - 1
                if 0 <= at < 16:
                    lift[j, out, low[row] * 16 + at] = 1
                    pair[j, par, row * 16 + at] = 1
                    if j != 1:
                        cot[j // 2, out, row * 16 + at] = 1
                else:
                    side = j // 2
                    for f in range(5):
                        cot_rim[side, f, out, f * 6 + row] = 1
                    for f in range(3):
                        lift_rim[side, f, out, f * 4 + low[row]] = 1
                        pair_rim[side, f, par, f * 6 + row] = 1
    edge_delta, edges, rims = zeros(64, 288), zeros(192, 672), zeros(112, 128)
    for side, col in ((0, 0), (1, 15)):
        for n in range(18):
            edge_delta[side * 32 + n, n * 16 + col] = 1
        for chunks, rows, src, at, corner in ((3, 2, 0, 0, 0), (2, 4, 288, 18, 9)):
            for q in range(chunks):
                for t in range(3):
                    here = src + q * rows * 48 + t * rows * 16 + col
                    for row in range(rows):
                        edges[side * 96 + at + (q * 3 + t) * rows + row, here + row * 16] = 1
                        if rows == 4 and t < 2:
                            edges[side * 96 + 80 + q * 8 + t * 4 + row, here + row * 16] = 1
                    edges[side * 96 + 48 + corner + q * 3 + t, here] = 1
                    edges[side * 96 + 64 + corner + q * 3 + t, here + (rows - 1) * 16] = 1
    for t in range(3):
        for q in range(3):
            rims[q * 16 + t * 4, 48 + q * 3 + t] = rims[q * 16 + t * 4 + 3, 64 + q * 3 + t] = 1
            for row in range(2):
                rims[q * 16 + t * 4 + 1 + row, q * 6 + t * 2 + row] = 1
        for q in range(2):
            for f, base, up, down in ((t, 18 + q * 12, 48, 64), (t + 3, 80 + q * 8, 96, 112)):
                if f < 5:
                    at = 48 + q * 32 + f * 6
                    rims[at, up + 9 + q * 3 + t] = rims[at + 5, down + 9 + q * 3 + t] = 1
                    for row in range(4):
                        rims[at + 1 + row, base + t * 4 + row] = 1
    parts = (widen, edges, rims, even_192, even_384, lift, lift_rim, cot, cot_rim, pair, pair_rim, edge_delta)
    return [jnp.asarray(p, BF) for p in parts]


def mm(a, b):
    return jnp.dot(a, b, preferred_element_type=F32)


def mm_nt(a, b):
    return lax.dot_general(a, b, (((1,), (1,)), ((), ())), preferred_element_type=F32)


def mm_tn(a, b):
    return lax.dot_general(a, b, (((0,), (0,)), ((), ())), preferred_element_type=F32)


def kernel(*refs):
    (latent_hbm, cot_hbm, gain_hbm, wr_hbm, wc_hbm), refs = refs[:5], refs[5:]
    const_hbm, (gi_ref, oc_ref, or_ref, og_ref), refs = refs[:12], refs[12:16], refs[16:]
    consts, refs = refs[:12], refs[12:]
    (widen, edges, rims, even_192, even_384, lift, lift_rim, cot, cot_rim, pair, pair_rim, edge_delta) = consts
    (
        latv, gain_v, wr, wc, sc, lc, lcp, hs, rim, hs_d, rim_d, sl, slp, xd, sd, fc, fr,
        g_core, g_x, g_y, sum_c, pw_c, pw_r, ws_c, ws_r, land_c, land_r, pack, flat_c, flat_r,
        load_sem, ssem, rsem, core_s, core_r, x_s, x_r, y_s, y_r, fin_s, fin_r,
        gc_s, gc_r, gx_s, gx_r, gy_s, gy_r,
    ), refs = refs[:47], refs[47:]
    bufs = [refs[5 * p : 5 * p + 5] for p in range(4)]
    yr_c, yr_r = refs[24:26]
    y_bufs = [(refs[20 + p], yr_c if p < 2 else yr_r) for p in range(4)]

    y, r, c = lax.axis_index("tm"), lax.axis_index("rows"), lax.axis_index("cols")
    h, zl = r % 2, r // 2
    x, zh = c % 4, c // 4
    z = zh * 4 + zl

    def dev(dy=0, dr=0, dc=0):
        return ((y + dy + 8) % 8, (r + dr + 8) % 8, (c + dc + 8) % 8)

    partner = (y, zl * 2 + 1 - h, c)

    def peer_x(o):
        return (y, r, zh * 4 + (x + o) % 4)

    f3, f2, late = pl.ds(0, 3), pl.ds(0, 2), pl.ds(3, 2)
    targets = [(latent_hbm, latv), (cot_hbm, sc.at[1, f3, pl.ds(1, 4)])]
    targets += list(zip(const_hbm, consts)) + [(gain_hbm, gain_v), (wr_hbm, wr), (wc_hbm, wc)]
    loads = [pltpu.make_async_copy(a, b, load_sem.at[n]) for n, (a, b) in enumerate(targets)]
    for copy in loads[:4]:
        copy.start()

    bar = pltpu.get_barrier_semaphore()
    sources = [dev(dy, dr, dc) for dc in (1, -1, 0) for dr in (-1, 0, 1) for dy in (0, 1) if (dy, dr, dc) != (0, 0, 0)]
    sources += [partner] + [peer_x(o) for o in range(1, 4)] + [dev(o) for o in range(1, 8)]
    for d in sources:
        pl.semaphore_signal(bar, inc=1, device_id=d, device_id_type=MESH)
    for q in range(8):
        src = (y, 2 * (q % 4) + r // 4, (q // 4) * 4 + r % 4)

        @pl.when(jnp.logical_or(src[1] != r, src[2] != c))
        def _():
            pl.semaphore_signal(bar, inc=1, device_id=src, device_id_type=MESH)

    mine = jnp.where(r == 4 * h + x, 1, 0)
    for copy in loads[4:]:
        copy.start()
    for copy in loads[:4]:
        copy.wait()

    own_low = latv[...].astype(F32).reshape(48, 384).astype(BF)
    own_low = mm(widen[...], own_low).astype(BF)
    lc[:, 1:3] = own_low.reshape(3, 2, 16, 384)
    own_cot = sc[1, 0:3, 1:5].reshape(192, 192)
    chunks = [own_low[:, 0:128], own_low[:, 128:256], own_low[:, 256:384], own_cot[:, 0:128]]
    chunks += [jnp.concatenate([own_cot[:, 128:192], jnp.zeros((192, 64), BF)], axis=1)]
    hs[...] = mm(edges[...], jnp.concatenate(chunks, axis=0)).astype(BF)

    pl.semaphore_wait(bar, len(sources) + 8 - mine)

    def inside(dy, dr, dc):
        ok = y >= 0
        for at, d in ((y, dy), (r, dr), (c, dc)):
            if d:
                ok = jnp.logical_and(ok, at < 7 if d > 0 else at > 0)
        return ok

    class Halo:
        def __init__(self, src, dst, n, *to):
            self.to, self.back = inside(*to), inside(*[-d for d in to])
            self.copy = pltpu.make_async_remote_copy(
                src_ref=src, dst_ref=dst, send_sem=ssem.at[n], recv_sem=rsem.at[n],
                device_id=dev(*to), device_id_type=MESH,
            )

        def start(self):
            pl.when(self.to)(self.copy.start)

        def wait(self):
            pl.when(self.to)(self.copy.wait_send)
            pl.when(self.back)(self.copy.wait_recv)

    halo = []
    for s, dc in ((0, -1), (1, 1)):
        tiles = ((0, 48, 0, 0, 0), (64, 16, 48, 0, 1), (48, 16, 64, 0, -1), (80, 16, 80, -1, 0), (64, 16, 96, -1, 1), (48, 16, 112, -1, -1))
        for n, (src, rows, dst, dy, dr) in enumerate(tiles):
            halo.append(Halo(hs.at[pl.ds(96 * s + src, rows)], rim.at[1 - s, pl.ds(dst, rows)], 11 + 6 * s + n, dy, dr, dc))
    halo += [
        Halo(lc.at[f3, 1], lc.at[f3, 3], 5, 0, -1, 0),
        Halo(lc.at[f3, 2], lc.at[f3, 0], 6, 0, 1, 0),
        Halo(sc.at[1, f3, 1], sc.at[1, f3, 5], 0, 0, -1, 0),
        Halo(sc.at[1, f3, 4], sc.at[1, f3, 0], 1, 0, 1, 0),
        Halo(sc.at[1, f2, pl.ds(1, 4)], sc.at[1, late, pl.ds(1, 4)], 2, -1, 0, 0),
        Halo(sc.at[1, f2, 1], sc.at[1, late, 5], 3, -1, -1, 0),
        Halo(sc.at[1, f2, 4], sc.at[1, late, 0], 4, -1, 1, 0),
    ]
    for copy in halo:
        copy.start()

    @pl.when(r == 0)
    def _():
        sc[1, :, 0] = jnp.zeros((5, 16, 192), BF)
        lc[:, 0] = jnp.zeros((3, 16, 384), BF)
        xd[:, 0] = jnp.zeros((3, 16, 192), BF)
        for n in (48, 96):
            rim[:, n : n + 16] = jnp.zeros((2, 16, 128), BF)

    @pl.when(r == 7)
    def _():
        sc[1, :, 5] = jnp.zeros((5, 16, 192), BF)
        lc[:, 3] = jnp.zeros((3, 16, 384), BF)
        xd[:, 5] = jnp.zeros((3, 16, 192), BF)
        for n in (64, 112):
            rim[:, n : n + 16] = jnp.zeros((2, 16, 128), BF)

    @pl.when(y == 7)
    def _():
        sc[1, 3:5] = jnp.zeros((2, 6, 16, 192), BF)
        rim[:, 80:128] = jnp.zeros((2, 48, 128), BF)

    @pl.when(c == 0)
    def _():
        rim[0] = jnp.zeros((128, 128), BF)
        rim_d[0] = jnp.zeros((32, 192), BF)

    @pl.when(c == 7)
    def _():
        rim[1] = jnp.zeros((128, 128), BF)
        rim_d[1] = jnp.zeros((32, 192), BF)

    for copy in loads[4:]:
        copy.wait()
    for copy in halo:
        copy.wait()

    rim_l, rim_c = [], []
    for s in range(2):
        near = mm(rims[...], rim[s]).astype(BF)
        rim_l.append(jnp.concatenate([near[0:16], near[16:32], near[32:48]], axis=1))
        rim_c.append(jnp.concatenate([near[48:80], near[80:112, 0:64]], axis=1))
    lcp[...] = mm(lc[...].reshape(192, 384), even_384[...]).astype(BF).reshape(3, 4, 16, 384)
    rim_p = [mm(rim_l[s], even_384[...]).astype(BF) for s in range(2)]
    for t in range(3):
        here = lc[t].reshape(64, 384)
        here_p = lcp[t].reshape(64, 384)
        for j in range(3):
            wide, wide_p = mm(lift[j], here), mm(lift[j], here_p)
            if j != 1:
                wide += mm(lift_rim[j // 2, t], rim_l[j // 2])
                wide_p += mm(lift_rim[j // 2, t], rim_p[j // 2])
            sl[j, t] = wide.astype(BF).reshape(6, 16, 384)
            slp[j, t] = wide_p.astype(BF).reshape(6, 16, 384)

    def fwd(i, total):
        for j in range(3):
            total += mm_nt(sl[j, :, pl.ds(i, 4)].reshape(192, 384), wr[i, j])
        return total

    z_float = lax.fori_loop(0, 3, fwd, jnp.zeros((192, 192), F32)).astype(BF).astype(F32)
    gain = gain_v[...]
    inverse = lax.rsqrt(jnp.mean(z_float * z_float, axis=-1, keepdims=True) + EPSILON)
    normed = z_float * inverse
    scaled = normed * gain
    sigma = 1.0 / (1.0 + jnp.exp(-scaled))
    hidden = (scaled * sigma).astype(BF)
    hidden_t = mm_nt(even_192[...], hidden).astype(BF)

    for f in range(5):
        here = sc[1, f].reshape(96, 192)
        for s in range(2):
            moved = mm(cot[s], here) + mm(cot_rim[s, f], rim_c[s])
            sc[2 * s, f] = moved.astype(BF).reshape(6, 16, 192)

    def cot_view(a, i, j):
        return sc[2 - j, pl.ds(2 - a, 3), pl.ds(2 - i, 4)].reshape(192, 192)

    def planes(both, half, dst, at):
        dst[0, pl.ds(at, half)] = both[:half, :128]
        dst[1, pl.ds(at, half)] = jnp.concatenate([both[:half, 128:], both[half:, :64]], axis=1)
        dst[2, pl.ds(at, half)] = both[half:, 64:]

    def conv_taps(n, carry):
        a, i = n // 3, n % 3
        for j in range(3):
            at = pl.multiple_of((n * 3 + j) * 96, 96)
            planes(mm(hidden_t, cot_view(a, i, j)), 96, fc, at)
        return carry

    lane_row = lax.broadcasted_iota(jnp.int32, (8, 128), 0)

    def block_c(hh, i, t):
        at = (81 * (t * 8 + 4 * hh + i)) // 2
        spare = jnp.zeros((8, 128), F32)
        for q in range(3):
            spare = jnp.where(lane_row == q, fc[q, pl.ds(at + 40, 1)], spare)
        return jnp.concatenate([fc[q, pl.ds(at, 40)] for q in range(3)] + [spare], axis=0)

    def block_r(hh, i, t):
        at = 27 * (t * 8 + 4 * hh + i)
        return jnp.concatenate([fr[q, pl.ds(at, 32)] for q in range(3)], axis=0)

    parts = [(block_c, 0, 4), (block_c, 4, 8), (block_r, 0, 4), (block_r, 4, 8)]

    def core_copy(p, o):
        bs, br = bufs[p][:2]
        i = (x + o) % 4
        return pltpu.make_async_remote_copy(
            src_ref=bs.at[i], dst_ref=br.at[i], send_sem=core_s.at[p * 4 + o],
            recv_sem=core_r.at[p * 4 + o], device_id=partner, device_id_type=MESH)

    def x_copy(p, m):
        xs, xr = bufs[p][2:4]
        return pltpu.make_async_remote_copy(
            src_ref=xs.at[m], dst_ref=xr.at[m], send_sem=x_s.at[p * 6 + m],
            recv_sem=x_r.at[p * 6 + m], device_id=peer_x(1 if m % 2 == 0 else 3), device_id_type=MESH)

    def core_send(p):
        block, lo, hi = parts[p]
        bs = bufs[p][0]
        for o in (2, 1, 3, 0):
            i = (x + o) % 4

            def fill(t, carry):
                bs[i, t - lo] = block(1 - h, i, t).astype(BF)
                return carry

            lax.fori_loop(lo, hi, fill, 0)
            core_copy(p, o).start()

    def x_fill(p, m, i, first, last, relayed):
        block, lo, _ = parts[p]
        _, br, xs, xr = bufs[p][:4]

        def fill(t, carry):
            total = block(h, i, t) + br[i, t - lo].astype(F32)
            if relayed:
                total += xr[m - 4, t - first].astype(F32)
            xs[m, t - first] = total.astype(BF)
            return carry

        lax.fori_loop(first, last, fill, 0)
        x_copy(p, m).start()

    def x_first(p):
        block, lo, hi = parts[p]
        mid = (lo + hi) // 2
        br, ac = bufs[p][1], bufs[p][4]
        core_copy(p, 2).wait()
        x_fill(p, 0, (x + 2) % 4, lo, mid, False)
        x_fill(p, 1, (x + 2) % 4, mid, hi, False)
        core_copy(p, 1).wait()
        x_fill(p, 2, (x + 1) % 4, mid, hi, False)
        core_copy(p, 3).wait()
        x_fill(p, 3, (x + 3) % 4, lo, mid, False)
        core_copy(p, 0).wait()

        def keep(t, carry):
            ac[t - lo] = block(h, x, t) + br[x, t - lo].astype(F32)
            return carry

        lax.fori_loop(lo, hi, keep, 0)

    def x_second(p):
        _, lo, hi = parts[p]
        mid = (lo + hi) // 2
        x_copy(p, 0).wait()
        x_fill(p, 4, (x + 1) % 4, lo, mid, True)
        x_copy(p, 1).wait()
        x_fill(p, 5, (x + 3) % 4, mid, hi, True)

    def y_copy(p, t):
        ys, yr = y_bufs[p]
        n = p * 4 + t - parts[p][1]
        return pltpu.make_async_remote_copy(
            src_ref=ys.at[t - parts[p][1]], dst_ref=yr.at[y], send_sem=y_s.at[n],
            recv_sem=y_r.at[p // 2 * 8 + y], device_id=(t, r, c), device_id_type=MESH)

    def y_send(p):
        _, lo, hi = parts[p]
        mid = (lo + hi) // 2
        xr, ac = bufs[p][3], bufs[p][4]
        ys = y_bufs[p][0]
        for m in range(2, 6):
            x_copy(p, m).wait()
        for first, last, one, two in ((lo, mid, 4, 3), (mid, hi, 5, 2)):

            def fill(t, carry):
                total = ac[t - lo] + xr[one, t - first].astype(F32) + xr[two, t - first].astype(F32)
                ac[t - lo] = total
                ys[t - lo] = total.astype(BF)
                return carry

            lax.fori_loop(first, last, fill, 0)
        for t in range(lo, hi):

            @pl.when(y != t)
            def _():
                y_copy(p, t).start()

    def y_wait_send(p):
        _, lo, hi = parts[p]
        for t in range(lo, hi):

            @pl.when(y != t)
            def _():
                y_copy(p, t).wait_send()

    def y_sum(p):
        _, lo, _ = parts[p]
        ac, yr = bufs[p][4], y_bufs[p][1]
        total = ac[y - lo]
        for o in range(1, 8):
            k = (y + o) % 8
            pltpu.make_async_copy(yr.at[k], yr.at[k], y_r.at[p // 2 * 8 + k]).wait()
            total += yr[k].astype(F32)
        return total

    lax.fori_loop(0, 5, conv_taps, 0)
    core_send(0)
    lax.fori_loop(5, 7, conv_taps, 0)
    x_first(0)
    lax.fori_loop(7, 9, conv_taps, 0)
    core_send(1)

    def back(n, total):
        a, i = n // 3, n % 3
        for j in range(3):
            total += mm_nt(cot_view(a, i, j), wc[a, i, j])
        return total

    hidden_grad = lax.fori_loop(0, 9, back, jnp.zeros((192, 192), F32))
    x_first(1)
    x_second(0)
    scaled_grad = hidden_grad * sigma * (1.0 + scaled * (1.0 - sigma))
    gain_local = jnp.sum(scaled_grad * normed, axis=0, keepdims=True)
    normed_grad = scaled_grad * gain
    delta = (
        inverse * (normed_grad - normed * jnp.mean(normed_grad * normed, axis=-1, keepdims=True))
    ).astype(BF)
    xd[:, 1:5] = delta.reshape(3, 4, 16, 192)
    rows_d = [
        Halo(xd.at[f3, 1], xd.at[f3, 5], 7, 0, -1, 0),
        Halo(xd.at[f3, 4], xd.at[f3, 0], 8, 0, 1, 0),
    ]
    for copy in rows_d:
        copy.start()

    tail = jnp.concatenate([gain_local[:, 128:], jnp.zeros((1, 64), F32)], axis=1)
    g_core[h] = jnp.where(lane_row == 0, gain_local[:, :128], jnp.where(lane_row == 1, tail, 0.0))

    def small(buf, at, ss, rs, n, to):
        return pltpu.make_async_remote_copy(
            src_ref=buf.at[at], dst_ref=buf.at[at], send_sem=ss.at[n], recv_sem=rs.at[n],
            device_id=to, device_id_type=MESH)

    g1 = small(g_core, h, gc_s, gc_r, 0, partner)
    g1.start()


    def lift_taps(n, carry):
        for j in range(3):
            at = pl.multiple_of((n * 3 + j) * 192, 192)
            view = slp[j, :, pl.ds(n, 4)].reshape(192, 384)
            planes(mm_tn(view, delta), 192, fr, at)
        return carry

    lax.fori_loop(0, 2, lift_taps, 0)
    core_send(2)
    x_second(1)
    lax.fori_loop(2, 3, lift_taps, 0)
    x_first(2)
    core_send(3)

    for copy in rows_d:
        copy.wait()

    hs_d[...] = mm(edge_delta[...], xd[...].reshape(288, 192)).astype(BF)
    cols_d = [
        Halo(hs_d.at[pl.ds(0, 32)], rim_d.at[1], 9, 0, 0, -1),
        Halo(hs_d.at[pl.ds(32, 32)], rim_d.at[0], 10, 0, 0, 1),
    ]
    for copy in cols_d:
        copy.start()

    g1.wait()
    g_x[x] = g_core[0] + g_core[1]
    g2 = [small(g_x, x, gx_s, gx_r, o - 1, peer_x(o)) for o in range(1, 4)]
    for copy in g2:
        copy.start()

    x_first(3)
    x_second(2)
    y_send(0)
    x_second(3)

    for copy in g2:
        copy.wait()
    g_y[y] = (g_x[0] + g_x[1]) + (g_x[2] + g_x[3])
    g3 = [small(g_y, y, gy_s, gy_r, o - 1, dev(o)) for o in range(1, 8)]
    for copy in g3:
        copy.start()

    y_send(1)
    y_send(2)

    for copy in cols_d:
        copy.wait()

    for t in range(3):
        here = xd[t].reshape(96, 192)
        for j in range(3):
            moved = mm(pair[j], here)
            if j != 1:
                moved += mm(pair_rim[j // 2, t], rim_d[j // 2])
            sd[j, t] = moved.astype(BF).reshape(6, 16, 192)

    def unlift(i, total):
        for j in range(3):
            total += mm(sd[2 - j, :, pl.ds(2 - i, 4)].reshape(192, 192), wr[i, j])
        return total

    lifted_grad = lax.fori_loop(0, 3, unlift, jnp.zeros((192, 384), F32))
    gi_ref[...] = lifted_grad.reshape(3, 2, 4, 8, 384).sum(axis=2).astype(BF)

    y_send(3)

    for copy in g3:
        copy.wait()
    g_sum = g_y[0]
    for k in range(1, 8):
        g_sum += g_y[k]
    g_hi = g_sum.astype(BF).astype(F32)
    g_lo = g_sum - g_hi

    extra = jnp.concatenate([g_hi[0:2], g_lo[0:2], jnp.zeros((4, 128), F32)], axis=0)

    def fin_copy(n, q):
        to = (y, 4 * h + x, q)
        src, dst = ((ws_c, land_c), (ws_r, land_r))[n]
        remote_one = pltpu.make_async_remote_copy(
            src_ref=src.at[q], dst_ref=dst.at[z], send_sem=fin_s.at[n * 8 + q], recv_sem=fin_r.at[n * 8 + z],
            device_id=to, device_id_type=MESH)
        return remote_one, jnp.logical_and(to[1] == r, q == c)

    def fin_start(n, q):
        remote_one, own = fin_copy(n, q)
        src, dst = ((ws_c, land_c), (ws_r, land_r))[n]

        @pl.when(jnp.logical_not(own))
        def _():
            remote_one.start()

        @pl.when(own)
        def _():
            pltpu.make_async_copy(src.at[q], dst.at[z], fin_r.at[n * 8 + z]).start()

    @pl.when(y < 4)
    def _():
        sum_c[...] = y_sum(0)

    @pl.when(y >= 4)
    def _():
        sum_c[...] = y_sum(1)

    pw_c[...] = jnp.zeros((3, 48, 128), F32)
    for q in range(3):
        pw_c[q, 0:40] = sum_c[40 * q : 40 * q + 40]
        pw_c[q, 40:41] = sum_c[120 + q : 121 + q]
    for q in range(8):
        rows = [pw_c[k, 5 * q : 5 * q + 8] for k in range(3)]
        ws_c[q] = jnp.concatenate(rows + [extra], axis=0).astype(BF)
        fin_start(0, q)

    @pl.when(y < 4)
    def _():
        pw_r[...] = y_sum(2).reshape(3, 32, 128)

    @pl.when(y >= 4)
    def _():
        pw_r[...] = y_sum(3).reshape(3, 32, 128)

    pack[...] = jnp.zeros((16, 128), F32)
    for q in range(8):
        low = (27 * q) // 8
        for k in range(3):
            pack[5 * k : 5 * k + 5] = pw_r[k, low : low + 5]
        ws_r[q] = pack[...].astype(BF)
        fin_start(1, q)

    def fin_sum(n):
        src, dst = ((ws_c, land_c), (ws_r, land_r))[n]
        total = jnp.zeros(dst.shape[1:], F32)
        for k in range(8):
            pltpu.make_async_copy(src.at[0], dst.at[k], fin_r.at[n * 8 + k]).wait()
            total += dst[k].astype(F32)
        return total

    flat_c[...] = jnp.zeros((24, 128), F32)
    flat_r[...] = jnp.zeros((24, 128), F32)
    total = fin_sum(0)
    og_ref[...] = total[24:26] + total[26:28]
    for k in range(3):
        for u in range(6):
            flat_c[3 * u + k : 3 * u + k + 1] = total[8 * k + u : 8 * k + u + 1]

    def cut(flat, off):
        lane = lax.broadcasted_iota(jnp.int32, (16, 128), 1)
        m, s = off // 128, off % 128
        turn = (128 - s) % 128
        one = pltpu.roll(flat[pl.ds(m, 16)], turn, 1)
        two = pltpu.roll(flat[pl.ds(m + 1, 16)], turn, 1)
        return jnp.where(lane < 128 - s, one, two)

    oc_ref[...] = cut(flat_c, 192 * (r % 2) + 24 * c)

    for p in range(4):
        y_wait_send(p)
    for n in range(2):
        for q in range(8):
            remote_one, own = fin_copy(n, q)

            @pl.when(jnp.logical_not(own))
            def _():
                remote_one.wait_send()

    total = fin_sum(1)
    for k in range(3):
        for u in range(5):
            flat_r[3 * u + k : 3 * u + k + 1] = total[5 * k + u : 5 * k + u + 1]
    or_ref[...] = cut(flat_r, 1296 * c - 384 * ((27 * c) // 8))


def hand_over(gi, oc, orr, og, gi_out, oc_out, or_out, og_out, sem):
    pairs = ((gi, gi_out), (oc, oc_out), (orr, or_out), (og, og_out))
    copies = [pltpu.make_async_copy(a, b, sem.at[n]) for n, (a, b) in enumerate(pairs)]
    for copy in copies:
        copy.start()
    for copy in copies:
        copy.wait()


def local(latent, cotangent, resample_weight, conv_weight, norm_gain):
    vm = pl.BlockSpec(memory_space=pltpu.VMEM)
    far = pl.BlockSpec(memory_space=pltpu.HBM)
    consts = selectors()
    dma, V = pltpu.SemaphoreType.DMA, pltpu.VMEM

    def reduce_buffers(n, tms):
        return [
            V((4, tms, n, 128), BF), V((4, tms, n, 128), BF), V((6, tms // 2, n, 128), BF),
            V((6, tms // 2, n, 128), BF), V((tms, n, 128), F32),
        ]

    scratch = [V(a.shape, BF) for a in consts]
    scratch += [
        V((3, 2, 8, 384), BF), V((1, 192), F32), V((3, 3, 192, 384), BF), V((3, 3, 3, 192, 192), BF),
        V((3, 5, 6, 16, 192), BF), V((3, 4, 16, 384), BF), V((3, 4, 16, 384), BF),
        V((192, 128), BF), V((2, 128, 128), BF), V((64, 192), BF), V((2, 32, 192), BF),
        V((3, 3, 6, 16, 384), BF), V((3, 3, 6, 16, 384), BF),
        V((3, 6, 16, 192), BF), V((3, 3, 6, 16, 192), BF),
        V((3, 2592 + 48, 128), F32), V((3, 1728 + 32, 128), F32),
        V((2, 8, 128), F32), V((4, 8, 128), F32), V((8, 8, 128), F32),
        V((128, 128), F32), V((3, 48, 128), F32), V((3, 32, 128), F32),
        V((8, 32, 128), BF), V((8, 16, 128), BF), V((8, 32, 128), BF), V((8, 16, 128), BF),
        V((16, 128), F32), V((24, 128), F32), V((24, 128), F32),
        dma((17,)), dma((23,)), dma((23,)), dma((16,)), dma((16,)), dma((24,)), dma((24,)), dma((16,)), dma((16,)),
        dma((16,)), dma((16,)), dma((1,)), dma((1,)), dma((3,)), dma((3,)), dma((7,)), dma((7,)),
        *reduce_buffers(128, 4), *reduce_buffers(128, 4), *reduce_buffers(96, 4), *reduce_buffers(96, 4),
        V((4, 128, 128), BF), V((4, 128, 128), BF), V((4, 96, 128), BF), V((4, 96, 128), BF), V((8, 128, 128), BF), V((8, 96, 128), BF),
    ]
    gi, oc, orr, og = pl.pallas_call(
        kernel,
        out_shape=[
            jax.ShapeDtypeStruct((3, 2, 8, 384), BF),
            jax.ShapeDtypeStruct((16, 128), F32),
            jax.ShapeDtypeStruct((16, 128), F32),
            jax.ShapeDtypeStruct((2, 128), F32),
        ],
        in_specs=[far] * (5 + len(consts)),
        out_specs=[vm] * 4,
        scratch_shapes=scratch,
        compiler_params=pltpu.CompilerParams(
            collective_id=0, has_side_effects=True, vmem_limit_bytes=56 * 2**20
        ),
        cost_estimate=pl.CostEstimate(flops=1_600_000_000, bytes_accessed=5_000_000, transcendentals=40_000),
    )(latent, cotangent, norm_gain.reshape(1, 192), jnp.swapaxes(resample_weight, 2, 3), conv_weight, *consts)
    shapes = [jax.ShapeDtypeStruct(a.shape, a.dtype) for a in (gi, oc, orr, og)]
    gi, oc, orr, og = pl.pallas_call(
        hand_over, out_shape=shapes, in_specs=[far] * 4, out_specs=[far] * 4, scratch_shapes=[dma((4,))]
    )(gi, oc, orr, og)
    return gi, orr.reshape(-1)[:1296], oc.reshape(-1)[:1944], og.reshape(-1)[:192]


def solution(mesh):
    in_specs = (P("tm", "rows", "cols", None), P("tm", "rows", "cols", None), P(), P(), P())
    out_specs = (
        P("tm", "rows", "cols", None),
        P(("tm", "rows", "cols")),
        P(("tm", "rows", "cols")),
        P(),
    )
    return jax.shard_map(local, mesh=mesh, in_specs=in_specs, out_specs=out_specs, check_vma=False)
```

```python
import functools

import jax
import jax.numpy as jnp
import numpy as np
from jax import lax
from jax.experimental import pallas as pl
from jax.experimental.pallas import tpu as pltpu
from jax.sharding import PartitionSpec as P

EPSILON = 1e-06
MESH = pl.DeviceIdType.MESH
BF = jnp.bfloat16
F32 = jnp.float32


def selectors():
    low = [0, 1, 1, 2, 2, 3]

    def zeros(*dims):
        return np.zeros(dims, np.float32)

    widen = zeros(96, 48)
    for t in range(3):
        for l in range(2):
            for c in range(16):
                widen[t * 32 + l * 16 + c, t * 16 + l * 8 + c // 2] = 1
    even_192, even_384 = zeros(192, 192), zeros(384, 384)
    for u in range(96):
        even_192[u, 2 * u] = even_192[96 + u, 2 * u + 1] = 1
    for u in range(192):
        even_384[2 * u, u] = even_384[2 * u + 1, 192 + u] = 1
    lift, lift_rim = zeros(3, 96, 64), zeros(2, 3, 96, 16)
    cot, cot_rim = zeros(2, 96, 96), zeros(2, 5, 96, 32)
    pair, pair_rim = zeros(3, 96, 96), zeros(2, 3, 96, 32)

    for row in range(6):
        for c in range(16):
            out = row * 16 + c
            par = row * 16 + (c % 2) * 8 + c // 2
            for j in range(3):
                at = c + j - 1
                if 0 <= at < 16:
                    lift[j, out, low[row] * 16 + at] = 1
                    pair[j, par, row * 16 + at] = 1
                    if j != 1:
                        cot[j // 2, out, row * 16 + at] = 1
                else:
                    side = j // 2
                    for f in range(5):
                        cot_rim[side, f, out, f * 6 + row] = 1
                    for f in range(3):
                        lift_rim[side, f, out, f * 4 + low[row]] = 1
                        pair_rim[side, f, par, f * 6 + row] = 1
    edge_delta, edges, rims = zeros(64, 288), zeros(192, 528), zeros(112, 128)
    for side, col in ((0, 0), (1, 15)):
        for n in range(18):
            edge_delta[side * 32 + n, n * 16 + col] = 1
        for chunks, rows, src, at, corner in ((3, 2, 0, 0, 0), (2, 4, 144, 18, 9)):
            wide, at_col = (8, col // 2) if rows == 2 else (16, col)
            for q in range(chunks):
                for t in range(3):
                    here = src + (q * 3 + t) * rows * wide + at_col
                    for row in range(rows):
                        edges[side * 96 + at + (q * 3 + t) * rows + row, here + row * wide] = 1
                        if rows == 4 and t < 2:
                            edges[side * 96 + 80 + q * 8 + t * 4 + row, here + row * wide] = 1
                    edges[side * 96 + 48 + corner + q * 3 + t, here] = 1
                    edges[side * 96 + 64 + corner + q * 3 + t, here + (rows - 1) * wide] = 1
    for t in range(3):
        for q in range(3):
            rims[q * 16 + t * 4, 48 + q * 3 + t] = rims[q * 16 + t * 4 + 3, 64 + q * 3 + t] = 1
            for row in range(2):
                rims[q * 16 + t * 4 + 1 + row, q * 6 + t * 2 + row] = 1
        for q in range(2):
            for f, base, up, down in ((t, 18 + q * 12, 48, 64), (t + 3, 80 + q * 8, 96, 112)):
                if f < 5:
                    at = 48 + q * 32 + f * 6
                    rims[at, up + 9 + q * 3 + t] = rims[at + 5, down + 9 + q * 3 + t] = 1
                    for row in range(4):
                        rims[at + 1 + row, base + t * 4 + row] = 1
    parts = (edges, even_384, widen, rims, even_192, lift, lift_rim, cot, cot_rim, pair, pair_rim, edge_delta)
    return [jnp.asarray(p, BF) for p in parts]


def mm(a, b):
    return jnp.dot(a, b, preferred_element_type=F32)


def mm_nt(a, b):
    return lax.dot_general(a, b, (((1,), (1,)), ((), ())), preferred_element_type=F32)


def mm_tn(a, b):
    return lax.dot_general(a, b, (((0,), (0,)), ((), ())), preferred_element_type=F32)


def kernel(*refs):
    (latent_hbm, cot_hbm, gain_hbm, wr_hbm, wc_hbm), refs = refs[:5], refs[5:]
    const_hbm, (gi_ref, oc_ref, or_ref, og_ref), refs = refs[:12], refs[12:16], refs[16:]
    consts, refs = refs[:12], refs[12:]
    (edges, even_384, widen, rims, even_192, lift, lift_rim, cot, cot_rim, pair, pair_rim, edge_delta) = consts
    (
        latv, gain_v, wr, wrp, wc, sc, lc, hs, rim, hs_d, rim_d, sl, xd, sd, fc, fr,
        g_core, g_x, g_y, sum_c, pw_c, pw_r, ws_c, ws_r, land_c, land_r, pack, flat_c, flat_r,
        load_sem, ssem, rsem, core_s, core_r, x_s, x_r, y_s, y_r, fin_s, fin_r,
        gc_s, gc_r, gx_s, gx_r, gy_s, gy_r,
    ), refs = refs[:46], refs[46:]
    bufs = [refs[5 * p : 5 * p + 5] for p in range(5)]
    yr_c, yr_r = refs[30:32]
    y_bufs = [(refs[25 + p], yr_c if p < 3 else yr_r) for p in range(5)]

    y, r, c = lax.axis_index("tm"), lax.axis_index("rows"), lax.axis_index("cols")
    h, zl = r % 2, r // 2
    x, zh = c % 4, c // 4
    z = zh * 4 + zl

    def dev(dy=0, dr=0, dc=0):
        return ((y + dy + 8) % 8, (r + dr + 8) % 8, (c + dc + 8) % 8)

    partner = (y, zl * 2 + 1 - h, c)

    def peer_x(o):
        return (y, r, zh * 4 + (x + o) % 4)

    f3, f2, late = pl.ds(0, 3), pl.ds(0, 2), pl.ds(3, 2)
    targets = [(latent_hbm, latv), (cot_hbm, sc.at[1, f3, pl.ds(1, 4)])]
    targets += list(zip(const_hbm, consts)) + [(gain_hbm, gain_v), (wr_hbm, wr), (wc_hbm, wc)]
    loads = [pltpu.make_async_copy(a, b, load_sem.at[n]) for n, (a, b) in enumerate(targets)]
    for copy in loads[:5]:
        copy.start()

    bar = pltpu.get_barrier_semaphore()
    sources = [dev(dy, dr, dc) for dc in (1, -1, 0) for dr in (-1, 0, 1) for dy in (0, 1) if (dy, dr, dc) != (0, 0, 0)]
    sources += [partner] + [peer_x(o) for o in range(1, 4)] + [dev(o) for o in range(1, 8)]
    for d in sources:
        pl.semaphore_signal(bar, inc=1, device_id=d, device_id_type=MESH)
    for q in range(8):
        src = (y, 2 * (q % 4) + r // 4, (q // 4) * 4 + r % 4)

        @pl.when(jnp.logical_or(src[1] != r, src[2] != c))
        def _():
            pl.semaphore_signal(bar, inc=1, device_id=src, device_id_type=MESH)

    mine = jnp.where(r == 4 * h + x, 1, 0)
    for copy in loads[:4]:
        copy.wait()

    own_low = mm(latv[...].astype(F32).reshape(48, 384).astype(BF), even_384[...]).astype(BF)
    own_cot = sc[1, 0:3, 1:5].reshape(192, 192)
    chunks = [own_low[:, 0:128], own_low[:, 128:256], own_low[:, 256:384], own_cot[:, 0:128]]
    chunks += [jnp.concatenate([own_cot[:, 128:192], jnp.zeros((192, 64), BF)], axis=1)]
    hs[...] = mm(edges[...], jnp.concatenate(chunks, axis=0)).astype(BF)

    pl.semaphore_wait(bar, len(sources) + 8 - mine)

    def inside(dy, dr, dc):
        ok = y >= 0
        for at, d in ((y, dy), (r, dr), (c, dc)):
            if d:
                ok = jnp.logical_and(ok, at < 7 if d > 0 else at > 0)
        return ok

    class Halo:
        def __init__(self, src, dst, n, *to):
            self.to, self.back = inside(*to), inside(*[-d for d in to])
            self.copy = pltpu.make_async_remote_copy(
                src_ref=src, dst_ref=dst, send_sem=ssem.at[n], recv_sem=rsem.at[n],
                device_id=dev(*to), device_id_type=MESH,
            )

        def start(self):
            pl.when(self.to)(self.copy.start)

        def wait(self):
            pl.when(self.to)(self.copy.wait_send)
            pl.when(self.back)(self.copy.wait_recv)

    halo = []
    for s, dc in ((0, -1), (1, 1)):
        tiles = ((0, 48, 0, 0, 0), (64, 16, 48, 0, 1), (48, 16, 64, 0, -1), (80, 16, 80, -1, 0), (64, 16, 96, -1, 1), (48, 16, 112, -1, -1))
        for n, (src, rows, dst, dy, dr) in enumerate(tiles):
            halo.append(Halo(hs.at[pl.ds(96 * s + src, rows)], rim.at[1 - s, pl.ds(dst, rows)], 11 + 6 * s + n, dy, dr, dc))
    for copy in halo:
        copy.start()
    loads[4].wait()
    lc[:, 1:3] = mm(widen[...], own_low).astype(BF).reshape(3, 2, 16, 384)
    halo += [
        Halo(lc.at[f3, 1], lc.at[f3, 3], 5, 0, -1, 0),
        Halo(lc.at[f3, 2], lc.at[f3, 0], 6, 0, 1, 0),
        Halo(sc.at[1, f3, 1], sc.at[1, f3, 5], 0, 0, -1, 0),
        Halo(sc.at[1, f3, 4], sc.at[1, f3, 0], 1, 0, 1, 0),
        Halo(sc.at[1, f2, pl.ds(1, 4)], sc.at[1, late, pl.ds(1, 4)], 2, -1, 0, 0),
        Halo(sc.at[1, f2, 1], sc.at[1, late, 5], 3, -1, -1, 0),
        Halo(sc.at[1, f2, 4], sc.at[1, late, 0], 4, -1, 1, 0),
    ]
    for copy in halo[12:] + loads[5:]:
        copy.start()

    @pl.when(r == 0)
    def _():
        sc[1, :, 0] = jnp.zeros((5, 16, 192), BF)
        lc[:, 0] = jnp.zeros((3, 16, 384), BF)
        xd[:, 0] = jnp.zeros((3, 16, 192), BF)
        for n in (48, 96):
            rim[:, n : n + 16] = jnp.zeros((2, 16, 128), BF)

    @pl.when(r == 7)
    def _():
        sc[1, :, 5] = jnp.zeros((5, 16, 192), BF)
        lc[:, 3] = jnp.zeros((3, 16, 384), BF)
        xd[:, 5] = jnp.zeros((3, 16, 192), BF)
        for n in (64, 112):
            rim[:, n : n + 16] = jnp.zeros((2, 16, 128), BF)

    @pl.when(y == 7)
    def _():
        sc[1, 3:5] = jnp.zeros((2, 6, 16, 192), BF)
        rim[:, 80:128] = jnp.zeros((2, 48, 128), BF)

    @pl.when(c == 0)
    def _():
        rim[0] = jnp.zeros((128, 128), BF)
        rim_d[0] = jnp.zeros((32, 192), BF)

    @pl.when(c == 7)
    def _():
        rim[1] = jnp.zeros((128, 128), BF)
        rim_d[1] = jnp.zeros((32, 192), BF)

    for copy in loads[5:]:
        copy.wait()

    def reorder(n, carry):
        wrp[n // 3, n % 3] = mm(wr[n // 3, n % 3], even_384[...]).astype(BF)
        return carry

    lax.fori_loop(0, 9, reorder, 0)
    for copy in halo:
        copy.wait()

    rim_l, rim_c = [], []
    for s in range(2):
        near = mm(rims[...], rim[s]).astype(BF)
        rim_l.append(jnp.concatenate([near[0:16], near[16:32], near[32:48]], axis=1))
        rim_c.append(jnp.concatenate([near[48:80], near[80:112, 0:64]], axis=1))
    for t in range(3):
        here = lc[t].reshape(64, 384)
        for j in range(3):
            wide = mm(lift[j], here)
            if j != 1:
                wide += mm(lift_rim[j // 2, t], rim_l[j // 2])
            sl[j, t] = wide.astype(BF).reshape(6, 16, 384)

    def fwd(i, total):
        for j in range(3):
            total += mm_nt(sl[j, :, pl.ds(i, 4)].reshape(192, 384), wrp[i, j])
        return total

    z_float = lax.fori_loop(0, 3, fwd, jnp.zeros((192, 192), F32)).astype(BF).astype(F32)
    gain = gain_v[...]
    inverse = lax.rsqrt(jnp.mean(z_float * z_float, axis=-1, keepdims=True) + EPSILON)
    normed = z_float * inverse
    scaled = normed * gain
    sigma = 1.0 / (1.0 + jnp.exp(-scaled))
    hidden = (scaled * sigma).astype(BF)
    hidden_t = mm_nt(even_192[...], hidden).astype(BF)

    for f in range(5):
        here = sc[1, f].reshape(96, 192)
        for s in range(2):
            moved = mm(cot[s], here) + mm(cot_rim[s, f], rim_c[s])
            sc[2 * s, f] = moved.astype(BF).reshape(6, 16, 192)

    def cot_view(a, i, j):
        return sc[2 - j, pl.ds(2 - a, 3), pl.ds(2 - i, 4)].reshape(192, 192)

    def planes(both, half, dst, at):
        dst[0, pl.ds(at, half)] = both[:half, :128]
        dst[1, pl.ds(at, half)] = jnp.concatenate([both[:half, 128:], both[half:, :64]], axis=1)
        dst[2, pl.ds(at, half)] = both[half:, 64:]

    def conv_tap(n, j):
        at = (n * 3 + j) * 96
        planes(mm(hidden_t, cot_view(n // 3, n % 3, j)), 96, fc, at if isinstance(n, int) else pl.multiple_of(at, 96))

    def conv_taps(n, carry):
        for j in range(3):
            conv_tap(n, j)
        return carry

    lane_row = lax.broadcasted_iota(jnp.int32, (8, 128), 0)

    def block_c(hh, i, t):
        at = (81 * (t * 8 + 4 * hh + i)) // 2
        spare = jnp.zeros((8, 128), F32)
        for q in range(3):
            spare = jnp.where(lane_row == q, fc[q, pl.ds(at + 40, 1)], spare)
        return jnp.concatenate([fc[q, pl.ds(at, 40)] for q in range(3)] + [spare], axis=0)

    def block_r(hh, i, t):
        at = 27 * (t * 8 + 4 * hh + i)
        return jnp.concatenate([fr[q, pl.ds(at, 32)] for q in range(3)], axis=0)

    parts = [
        (block_c, (0, 1)), (block_c, (3, 6)), (block_c, (2, 4, 5, 7)),
        (block_r, (0, 2, 4, 6)), (block_r, (1, 3, 5, 7)),
    ]

    def halves(p):
        tms = list(enumerate(parts[p][1]))
        return tms[: len(tms) // 2], tms[len(tms) // 2 :]

    def core_copy(p, o):
        bs, br = bufs[p][:2]
        i = (x + o) % 4
        return pltpu.make_async_remote_copy(
            src_ref=bs.at[i], dst_ref=br.at[i], send_sem=core_s.at[p * 4 + o],
            recv_sem=core_r.at[p * 4 + o], device_id=partner, device_id_type=MESH)

    def x_copy(p, m):
        xs, xr = bufs[p][2:4]
        return pltpu.make_async_remote_copy(
            src_ref=xs.at[m], dst_ref=xr.at[m], send_sem=x_s.at[p * 6 + m],
            recv_sem=x_r.at[p * 6 + m], device_id=peer_x(1 if m % 2 == 0 else 3), device_id_type=MESH)

    def core_send(p):
        block, tms = parts[p]
        bs = bufs[p][0]
        for o in (2, 1, 3, 0):
            i = (x + o) % 4
            for n, t in enumerate(tms):
                bs[i, n] = block(1 - h, i, t).astype(BF)
            core_copy(p, o).start()

    def x_fill(p, m, i, half, relayed):
        block = parts[p][0]
        _, br, xs, xr = bufs[p][:4]
        for k, (n, t) in enumerate(half):
            total = block(h, i, t) + br[i, n].astype(F32)
            if relayed:
                total += xr[m - 4, k].astype(F32)
            xs[m, k] = total.astype(BF)
        x_copy(p, m).start()

    def x_first(p):
        block, tms = parts[p]
        one, two = halves(p)
        br, ac = bufs[p][1], bufs[p][4]
        core_copy(p, 2).wait()
        x_fill(p, 0, (x + 2) % 4, one, False)
        x_fill(p, 1, (x + 2) % 4, two, False)
        core_copy(p, 1).wait()
        x_fill(p, 2, (x + 1) % 4, two, False)
        core_copy(p, 3).wait()
        x_fill(p, 3, (x + 3) % 4, one, False)
        core_copy(p, 0).wait()
        for n, t in enumerate(tms):
            ac[n] = block(h, x, t) + br[x, n].astype(F32)

    def x_second(p):
        one, two = halves(p)
        x_copy(p, 0).wait()
        x_fill(p, 4, (x + 1) % 4, one, True)
        x_copy(p, 1).wait()
        x_fill(p, 5, (x + 3) % 4, two, True)

    def y_copy(p, n):
        t = parts[p][1][n]
        ys, yr = y_bufs[p]
        return pltpu.make_async_remote_copy(
            src_ref=ys.at[n], dst_ref=yr.at[y], send_sem=y_s.at[p // 3 * 8 + t],
            recv_sem=y_r.at[p // 3 * 8 + y], device_id=(t, r, c), device_id_type=MESH)

    def y_send(p):
        xr, ac, ys = bufs[p][3], bufs[p][4], y_bufs[p][0]
        for m in range(2, 6):
            x_copy(p, m).wait()
        for half, one, two in zip(halves(p), (4, 5), (3, 2)):
            for k, (n, t) in enumerate(half):
                total = ac[n] + xr[one, k].astype(F32) + xr[two, k].astype(F32)
                ac[n] = total
                ys[n] = total.astype(BF)
        for n, t in enumerate(parts[p][1]):

            @pl.when(y != t)
            def _():
                y_copy(p, n).start()

    def y_wait_send(p):
        for n, t in enumerate(parts[p][1]):

            @pl.when(y != t)
            def _():
                y_copy(p, n).wait_send()

    def y_sum(p, dst):
        ac, yr = bufs[p][4], y_bufs[p][1]
        at = 0
        for n, t in enumerate(parts[p][1]):
            at = jnp.where(y == t, n + 1, at)

        @pl.when(at > 0)
        def _():
            total = ac[at - 1]
            for o in range(1, 8):
                k = (y + o) % 8
                pltpu.make_async_copy(yr.at[k], yr.at[k], y_r.at[p // 3 * 8 + k]).wait()
                total += yr[k].astype(F32)
            dst[...] = total.reshape(dst.shape)

    lax.fori_loop(0, 2, conv_taps, 0)
    conv_tap(2, 0)
    core_send(0)
    conv_tap(2, 1)
    conv_tap(2, 2)
    conv_taps(3, 0)
    lax.fori_loop(4, 9, conv_taps, 0)
    core_send(1)
    core_send(2)
    x_first(0)
    x_first(1)

    def back(n, total):
        a, i = n // 3, n % 3
        for j in range(3):
            total += mm_nt(cot_view(a, i, j), wc[a, i, j])
        return total

    hidden_grad = lax.fori_loop(0, 9, back, jnp.zeros((192, 192), F32))
    scaled_grad = hidden_grad * sigma * (1.0 + scaled * (1.0 - sigma))
    gain_local = jnp.sum(scaled_grad * normed, axis=0, keepdims=True)
    normed_grad = scaled_grad * gain
    delta = (
        inverse * (normed_grad - normed * jnp.mean(normed_grad * normed, axis=-1, keepdims=True))
    ).astype(BF)
    xd[:, 1:5] = delta.reshape(3, 4, 16, 192)
    rows_d = [
        Halo(xd.at[f3, 1], xd.at[f3, 5], 7, 0, -1, 0),
        Halo(xd.at[f3, 4], xd.at[f3, 0], 8, 0, 1, 0),
    ]
    for copy in rows_d:
        copy.start()

    tail = jnp.concatenate([gain_local[:, 128:], jnp.zeros((1, 64), F32)], axis=1)
    g_core[h] = jnp.where(lane_row == 0, gain_local[:, :128], jnp.where(lane_row == 1, tail, 0.0))

    def small(buf, at, ss, rs, n, to):
        return pltpu.make_async_remote_copy(
            src_ref=buf.at[at], dst_ref=buf.at[at], send_sem=ss.at[n], recv_sem=rs.at[n],
            device_id=to, device_id_type=MESH)

    g1 = small(g_core, h, gc_s, gc_r, 0, partner)
    g1.start()
    x_first(2)


    def lift_taps(n, carry):
        for j in range(3):
            at = pl.multiple_of((n * 3 + j) * 192, 192)
            view = sl[j, :, pl.ds(n, 4)].reshape(192, 384)
            planes(mm_tn(view, delta), 192, fr, at)
        return carry

    lax.fori_loop(0, 3, lift_taps, 0)
    core_send(3)
    core_send(4)
    for copy in rows_d:
        copy.wait()
    hs_d[...] = mm(edge_delta[...], xd[...].reshape(288, 192)).astype(BF)
    cols_d = [
        Halo(hs_d.at[pl.ds(0, 32)], rim_d.at[1], 9, 0, 0, -1),
        Halo(hs_d.at[pl.ds(32, 32)], rim_d.at[0], 10, 0, 0, 1),
    ]
    for copy in cols_d:
        copy.start()

    g1.wait()
    g_x[x] = g_core[0] + g_core[1]
    g2 = [small(g_x, x, gx_s, gx_r, o - 1, peer_x(o)) for o in range(1, 4)]
    for copy in g2:
        copy.start()

    x_second(0)
    x_second(1)
    x_first(3)
    x_first(4)
    x_second(2)
    y_send(0)
    y_send(1)
    x_second(3)
    for copy in g2:
        copy.wait()
    g_y[y] = (g_x[0] + g_x[1]) + (g_x[2] + g_x[3])
    g3 = [small(g_y, y, gy_s, gy_r, o - 1, dev(o)) for o in range(1, 8)]
    for copy in g3:
        copy.start()
    x_second(4)
    y_send(2)
    y_send(3)
    y_send(4)

    for copy in cols_d:
        copy.wait()

    for t in range(3):
        here = xd[t].reshape(96, 192)
        for j in range(3):
            moved = mm(pair[j], here)
            if j != 1:
                moved += mm(pair_rim[j // 2, t], rim_d[j // 2])
            sd[j, t] = moved.astype(BF).reshape(6, 16, 192)

    def unlift(i, total):
        for j in range(3):
            total += mm(sd[2 - j, :, pl.ds(2 - i, 4)].reshape(192, 192), wr[i, j])
        return total

    lifted_grad = lax.fori_loop(0, 3, unlift, jnp.zeros((192, 384), F32))
    gi_ref[...] = lifted_grad.reshape(3, 2, 4, 8, 384).sum(axis=2).astype(BF)


    for copy in g3:
        copy.wait()
    g_sum = g_y[0]
    for k in range(1, 8):
        g_sum += g_y[k]
    g_hi = g_sum.astype(BF).astype(F32)
    g_lo = g_sum - g_hi

    extra = jnp.concatenate([g_hi[0:2], g_lo[0:2], jnp.zeros((4, 128), F32)], axis=0)

    def fin_copy(n, q):
        to = (y, 4 * h + x, q)
        src, dst = ((ws_c, land_c), (ws_r, land_r))[n]
        remote_one = pltpu.make_async_remote_copy(
            src_ref=src.at[q], dst_ref=dst.at[z], send_sem=fin_s.at[n * 8 + q], recv_sem=fin_r.at[n * 8 + z],
            device_id=to, device_id_type=MESH)
        return remote_one, jnp.logical_and(to[1] == r, q == c)

    def fin_start(n, q):
        remote_one, own = fin_copy(n, q)
        src, dst = ((ws_c, land_c), (ws_r, land_r))[n]

        @pl.when(jnp.logical_not(own))
        def _():
            remote_one.start()

        @pl.when(own)
        def _():
            pltpu.make_async_copy(src.at[q], dst.at[z], fin_r.at[n * 8 + z]).start()

    for p in range(3):
        y_sum(p, sum_c)
    pw_c[...] = jnp.zeros((3, 48, 128), F32)
    for q in range(3):
        pw_c[q, 0:40] = sum_c[40 * q : 40 * q + 40]
        pw_c[q, 40:41] = sum_c[120 + q : 121 + q]
    for q in range(8):
        rows = [pw_c[k, 5 * q : 5 * q + 8] for k in range(3)]
        ws_c[q] = jnp.concatenate(rows + [extra], axis=0).astype(BF)
        fin_start(0, q)

    y_sum(3, pw_r)
    y_sum(4, pw_r)
    pack[...] = jnp.zeros((16, 128), F32)
    for q in range(8):
        low = (27 * q) // 8
        for k in range(3):
            pack[5 * k : 5 * k + 5] = pw_r[k, low : low + 5]
        ws_r[q] = pack[...].astype(BF)
        fin_start(1, q)

    def fin_sum(n):
        src, dst = ((ws_c, land_c), (ws_r, land_r))[n]
        total = jnp.zeros(dst.shape[1:], F32)
        for k in range(8):
            pltpu.make_async_copy(src.at[0], dst.at[k], fin_r.at[n * 8 + k]).wait()
            total += dst[k].astype(F32)
        return total

    flat_c[...] = jnp.zeros((24, 128), F32)
    flat_r[...] = jnp.zeros((24, 128), F32)
    total = fin_sum(0)
    og_ref[...] = total[24:26] + total[26:28]
    for k in range(3):
        for u in range(6):
            flat_c[3 * u + k : 3 * u + k + 1] = total[8 * k + u : 8 * k + u + 1]

    def cut(flat, off):
        lane = lax.broadcasted_iota(jnp.int32, (16, 128), 1)
        m, s = off // 128, off % 128
        turn = (128 - s) % 128
        one = pltpu.roll(flat[pl.ds(m, 16)], turn, 1)
        two = pltpu.roll(flat[pl.ds(m + 1, 16)], turn, 1)
        return jnp.where(lane < 128 - s, one, two)

    oc_ref[...] = cut(flat_c, 192 * (r % 2) + 24 * c)

    for p in range(5):
        y_wait_send(p)
    for n in range(2):
        for q in range(8):
            remote_one, own = fin_copy(n, q)

            @pl.when(jnp.logical_not(own))
            def _():
                remote_one.wait_send()

    total = fin_sum(1)
    for k in range(3):
        for u in range(5):
            flat_r[3 * u + k : 3 * u + k + 1] = total[5 * k + u : 5 * k + u + 1]
    or_ref[...] = cut(flat_r, 1296 * c - 384 * ((27 * c) // 8))


def hand_over(gi, oc, orr, og, gi_out, oc_out, or_out, og_out):
    gi_out[...], oc_out[...], or_out[...], og_out[...] = gi[...], oc[...], orr[...], og[...]


def local(latent, cotangent, resample_weight, conv_weight, norm_gain):
    vm = pl.BlockSpec(memory_space=pltpu.VMEM)
    far = pl.BlockSpec(memory_space=pltpu.HBM)
    consts = selectors()
    dma, V = pltpu.SemaphoreType.DMA, pltpu.VMEM

    def reduce_buffers(n, tms):
        return [
            V((4, tms, n, 128), BF), V((4, tms, n, 128), BF), V((6, tms // 2, n, 128), BF),
            V((6, tms // 2, n, 128), BF), V((tms, n, 128), F32),
        ]

    scratch = [V(a.shape, BF) for a in consts]
    scratch += [
        V((3, 2, 8, 384), BF), V((1, 192), F32), V((3, 3, 192, 384), BF), V((3, 3, 192, 384), BF),
        V((3, 3, 3, 192, 192), BF),
        V((3, 5, 6, 16, 192), BF), V((3, 4, 16, 384), BF),
        V((192, 128), BF), V((2, 128, 128), BF), V((64, 192), BF), V((2, 32, 192), BF),
        V((3, 3, 6, 16, 384), BF),
        V((3, 6, 16, 192), BF), V((3, 3, 6, 16, 192), BF),
        V((3, 2592 + 48, 128), F32), V((3, 1728 + 32, 128), F32),
        V((2, 8, 128), F32), V((4, 8, 128), F32), V((8, 8, 128), F32),
        V((128, 128), F32), V((3, 48, 128), F32), V((3, 32, 128), F32),
        V((8, 32, 128), BF), V((8, 16, 128), BF), V((8, 32, 128), BF), V((8, 16, 128), BF),
        V((16, 128), F32), V((24, 128), F32), V((24, 128), F32),
        dma((17,)), dma((23,)), dma((23,)), dma((20,)), dma((20,)), dma((30,)), dma((30,)), dma((16,)), dma((16,)),
        dma((16,)), dma((16,)), dma((1,)), dma((1,)), dma((3,)), dma((3,)), dma((7,)), dma((7,)),
        *reduce_buffers(128, 2), *reduce_buffers(128, 2), *reduce_buffers(128, 4),
        *reduce_buffers(96, 4), *reduce_buffers(96, 4),
        V((2, 128, 128), BF), V((2, 128, 128), BF), V((4, 128, 128), BF), V((4, 96, 128), BF), V((4, 96, 128), BF), V((8, 128, 128), BF), V((8, 96, 128), BF),
    ]
    gi, oc, orr, og = pl.pallas_call(
        kernel,
        out_shape=[
            jax.ShapeDtypeStruct((3, 2, 8, 384), BF),
            jax.ShapeDtypeStruct((16, 128), F32),
            jax.ShapeDtypeStruct((16, 128), F32),
            jax.ShapeDtypeStruct((2, 128), F32),
        ],
        in_specs=[far] * (5 + len(consts)),
        out_specs=[vm] * 4,
        scratch_shapes=scratch,
        compiler_params=pltpu.CompilerParams(
            collective_id=0, has_side_effects=True, vmem_limit_bytes=56 * 2**20
        ),
        cost_estimate=pl.CostEstimate(flops=1_600_000_000, bytes_accessed=5_000_000, transcendentals=40_000),
    )(latent, cotangent, norm_gain.reshape(1, 192), jnp.swapaxes(resample_weight, 2, 3), conv_weight, *consts)
    shapes = [jax.ShapeDtypeStruct(a.shape, a.dtype) for a in (gi, oc, orr, og)]
    gi, oc, orr, og = pl.pallas_call(
        hand_over, out_shape=shapes, in_specs=[vm] * 4, out_specs=[vm] * 4
    )(gi, oc, orr, og)
    return gi, orr.reshape(-1)[:1296], oc.reshape(-1)[:1944], og.reshape(-1)[:192]


def solution(mesh):
    in_specs = (P("tm", "rows", "cols", None), P("tm", "rows", "cols", None), P(), P(), P())
    out_specs = (
        P("tm", "rows", "cols", None),
        P(("tm", "rows", "cols")),
        P(("tm", "rows", "cols")),
        P(),
    )
    return jax.shard_map(local, mesh=mesh, in_specs=in_specs, out_specs=out_specs, check_vma=False)
```

```python
import functools

import jax
import jax.numpy as jnp
import numpy as np
from jax import lax
from jax.experimental import pallas as pl
from jax.experimental.pallas import tpu as pltpu
from jax.sharding import PartitionSpec as P

EPSILON = 1e-06
MESH = pl.DeviceIdType.MESH
BF = jnp.bfloat16
F32 = jnp.float32


def selectors():
    low = [0, 1, 1, 2, 2, 3]

    def zeros(*dims):
        return np.zeros(dims, np.float32)

    widen = zeros(96, 48)
    for t in range(3):
        for l in range(2):
            for c in range(16):
                widen[t * 32 + l * 16 + c, t * 16 + l * 8 + c // 2] = 1
    even_192, even_384 = zeros(192, 192), zeros(384, 384)
    for u in range(96):
        even_192[u, 2 * u] = even_192[96 + u, 2 * u + 1] = 1
    for u in range(192):
        even_384[2 * u, u] = even_384[2 * u + 1, 192 + u] = 1
    lift, lift_rim = zeros(3, 96, 64), zeros(2, 3, 96, 16)
    cot, cot_rim = zeros(2, 96, 96), zeros(2, 5, 96, 32)
    pair, pair_rim = zeros(3, 96, 96), zeros(2, 3, 96, 32)

    for row in range(6):
        for c in range(16):
            out = row * 16 + c
            par = row * 16 + (c % 2) * 8 + c // 2
            for j in range(3):
                at = c + j - 1
                if 0 <= at < 16:
                    lift[j, out, low[row] * 16 + at] = 1
                    pair[j, par, row * 16 + at] = 1
                    if j != 1:
                        cot[j // 2, out, row * 16 + at] = 1
                else:
                    side = j // 2
                    for f in range(5):
                        cot_rim[side, f, out, f * 6 + row] = 1
                    for f in range(3):
                        lift_rim[side, f, out, f * 4 + low[row]] = 1
                        pair_rim[side, f, par, f * 6 + row] = 1
    edge_delta, edges, rims = zeros(64, 288), zeros(192, 528), zeros(112, 128)
    for side, col in ((0, 0), (1, 15)):
        for n in range(18):
            edge_delta[side * 32 + n, n * 16 + col] = 1
        for chunks, rows, src, at, corner in ((3, 2, 0, 0, 0), (2, 4, 144, 18, 9)):
            wide, at_col = (8, col // 2) if rows == 2 else (16, col)
            for q in range(chunks):
                for t in range(3):
                    here = src + (q * 3 + t) * rows * wide + at_col
                    for row in range(rows):
                        edges[side * 96 + at + (q * 3 + t) * rows + row, here + row * wide] = 1
                        if rows == 4 and t < 2:
                            edges[side * 96 + 80 + q * 8 + t * 4 + row, here + row * wide] = 1
                    edges[side * 96 + 48 + corner + q * 3 + t, here] = 1
                    edges[side * 96 + 64 + corner + q * 3 + t, here + (rows - 1) * wide] = 1
    for t in range(3):
        for q in range(3):
            rims[q * 16 + t * 4, 48 + q * 3 + t] = rims[q * 16 + t * 4 + 3, 64 + q * 3 + t] = 1
            for row in range(2):
                rims[q * 16 + t * 4 + 1 + row, q * 6 + t * 2 + row] = 1
        for q in range(2):
            for f, base, up, down in ((t, 18 + q * 12, 48, 64), (t + 3, 80 + q * 8, 96, 112)):
                if f < 5:
                    at = 48 + q * 32 + f * 6
                    rims[at, up + 9 + q * 3 + t] = rims[at + 5, down + 9 + q * 3 + t] = 1
                    for row in range(4):
                        rims[at + 1 + row, base + t * 4 + row] = 1
    parts = (edges, even_384, widen, rims, even_192, lift, lift_rim, cot, cot_rim, pair, pair_rim, edge_delta)
    return [jnp.asarray(p, BF) for p in parts]


def mm(a, b):
    return jnp.dot(a, b, preferred_element_type=F32)


def mm_nt(a, b):
    return lax.dot_general(a, b, (((1,), (1,)), ((), ())), preferred_element_type=F32)


def mm_tn(a, b):
    return lax.dot_general(a, b, (((0,), (0,)), ((), ())), preferred_element_type=F32)


def kernel(*refs):
    (latent_hbm, cot_hbm, gain_hbm, wr_hbm, wc_hbm), refs = refs[:5], refs[5:]
    const_hbm, (gi_ref, oc_ref, or_ref, og_ref), refs = refs[:12], refs[12:16], refs[16:]
    consts, refs = refs[:12], refs[12:]
    (edges, even_384, widen, rims, even_192, lift, lift_rim, cot, cot_rim, pair, pair_rim, edge_delta) = consts
    (
        latv, gain_v, wr, wrp, wc, sc, lc, hs, rim, hs_d, rim_d, sl, xd, sd, fc, fr,
        g_core, g_x, g_y, sum_c, pw_c, pw_r, ws_c, ws_r, land_c, land_r, pack, flat_c, flat_r,
        load_sem, ssem, rsem, core_s, core_r, x_s, x_r, y_s, y_r, fin_s, fin_r,
        gc_s, gc_r, gx_s, gx_r, gy_s, gy_r,
    ), refs = refs[:46], refs[46:]
    bufs = [refs[5 * p : 5 * p + 5] for p in range(5)]
    yr_c, yr_r = refs[30:32]
    y_bufs = [(refs[25 + p], yr_c if p < 3 else yr_r) for p in range(5)]

    y, r, c = lax.axis_index("tm"), lax.axis_index("rows"), lax.axis_index("cols")
    h, zl = r % 2, r // 2
    x, zh = c % 4, c // 4
    z = zh * 4 + zl

    def dev(dy=0, dr=0, dc=0):
        return ((y + dy + 8) % 8, (r + dr + 8) % 8, (c + dc + 8) % 8)

    partner = (y, zl * 2 + 1 - h, c)

    def peer_x(o):
        return (y, r, zh * 4 + (x + o) % 4)

    f3, f2, late = pl.ds(0, 3), pl.ds(0, 2), pl.ds(3, 2)
    targets = [(latent_hbm, latv), (cot_hbm, sc.at[1, f3, pl.ds(1, 4)])]
    targets += list(zip(const_hbm, consts)) + [(gain_hbm, gain_v), (wr_hbm, wr), (wc_hbm, wc)]
    loads = [pltpu.make_async_copy(a, b, load_sem.at[n]) for n, (a, b) in enumerate(targets)]
    for copy in loads[:5]:
        copy.start()

    bar = pltpu.get_barrier_semaphore()
    sources = [dev(dy, dr, dc) for dc in (1, -1, 0) for dr in (-1, 0, 1) for dy in (0, 1) if (dy, dr, dc) != (0, 0, 0)]
    sources += [partner] + [peer_x(o) for o in range(1, 4)] + [dev(o) for o in range(1, 8)]
    for d in sources:
        pl.semaphore_signal(bar, inc=1, device_id=d, device_id_type=MESH)
    for q in range(8):
        src = (y, 2 * (q % 4) + r // 4, (q // 4) * 4 + r % 4)

        @pl.when(jnp.logical_or(src[1] != r, src[2] != c))
        def _():
            pl.semaphore_signal(bar, inc=1, device_id=src, device_id_type=MESH)

    mine = jnp.where(r == 4 * h + x, 1, 0)
    for copy in loads[:4]:
        copy.wait()

    own_low = mm(latv[...].astype(F32).reshape(48, 384).astype(BF), even_384[...]).astype(BF)
    own_cot = sc[1, 0:3, 1:5].reshape(192, 192)
    chunks = [own_low[:, 0:128], own_low[:, 128:256], own_low[:, 256:384], own_cot[:, 0:128]]
    chunks += [jnp.concatenate([own_cot[:, 128:192], jnp.zeros((192, 64), BF)], axis=1)]
    hs[...] = mm(edges[...], jnp.concatenate(chunks, axis=0)).astype(BF)

    pl.semaphore_wait(bar, len(sources) + 8 - mine)

    def inside(dy, dr, dc):
        ok = y >= 0
        for at, d in ((y, dy), (r, dr), (c, dc)):
            if d:
                ok = jnp.logical_and(ok, at < 7 if d > 0 else at > 0)
        return ok

    class Halo:
        def __init__(self, src, dst, n, *to):
            self.to, self.back = inside(*to), inside(*[-d for d in to])
            self.copy = pltpu.make_async_remote_copy(
                src_ref=src, dst_ref=dst, send_sem=ssem.at[n], recv_sem=rsem.at[n],
                device_id=dev(*to), device_id_type=MESH,
            )

        def start(self):
            pl.when(self.to)(self.copy.start)

        def wait(self):
            pl.when(self.to)(self.copy.wait_send)
            pl.when(self.back)(self.copy.wait_recv)

    halo = []
    for s, dc in ((0, -1), (1, 1)):
        tiles = ((0, 48, 0, 0, 0), (64, 16, 48, 0, 1), (48, 16, 64, 0, -1), (80, 16, 80, -1, 0), (64, 16, 96, -1, 1), (48, 16, 112, -1, -1))
        for n, (src, rows, dst, dy, dr) in enumerate(tiles):
            halo.append(Halo(hs.at[pl.ds(96 * s + src, rows)], rim.at[1 - s, pl.ds(dst, rows)], 11 + 6 * s + n, dy, dr, dc))
    for copy in halo:
        copy.start()
    loads[4].wait()
    lc[:, 1:3] = mm(widen[...], own_low).astype(BF).reshape(3, 2, 16, 384)
    halo += [
        Halo(lc.at[f3, 1], lc.at[f3, 3], 5, 0, -1, 0),
        Halo(lc.at[f3, 2], lc.at[f3, 0], 6, 0, 1, 0),
        Halo(sc.at[1, f3, 1], sc.at[1, f3, 5], 0, 0, -1, 0),
        Halo(sc.at[1, f3, 4], sc.at[1, f3, 0], 1, 0, 1, 0),
        Halo(sc.at[1, f2, pl.ds(1, 4)], sc.at[1, late, pl.ds(1, 4)], 2, -1, 0, 0),
        Halo(sc.at[1, f2, 1], sc.at[1, late, 5], 3, -1, -1, 0),
        Halo(sc.at[1, f2, 4], sc.at[1, late, 0], 4, -1, 1, 0),
    ]
    for copy in halo[12:] + loads[5:]:
        copy.start()

    @pl.when(r == 0)
    def _():
        sc[1, :, 0] = jnp.zeros((5, 16, 192), BF)
        lc[:, 0] = jnp.zeros((3, 16, 384), BF)
        xd[:, 0] = jnp.zeros((3, 16, 192), BF)
        for n in (48, 96):
            rim[:, n : n + 16] = jnp.zeros((2, 16, 128), BF)

    @pl.when(r == 7)
    def _():
        sc[1, :, 5] = jnp.zeros((5, 16, 192), BF)
        lc[:, 3] = jnp.zeros((3, 16, 384), BF)
        xd[:, 5] = jnp.zeros((3, 16, 192), BF)
        for n in (64, 112):
            rim[:, n : n + 16] = jnp.zeros((2, 16, 128), BF)

    @pl.when(y == 7)
    def _():
        sc[1, 3:5] = jnp.zeros((2, 6, 16, 192), BF)
        rim[:, 80:128] = jnp.zeros((2, 48, 128), BF)

    @pl.when(c == 0)
    def _():
        rim[0] = jnp.zeros((128, 128), BF)
        rim_d[0] = jnp.zeros((32, 192), BF)

    @pl.when(c == 7)
    def _():
        rim[1] = jnp.zeros((128, 128), BF)
        rim_d[1] = jnp.zeros((32, 192), BF)

    for copy in loads[5:]:
        copy.wait()

    def reorder(n, carry):
        wrp[n // 3, n % 3] = mm(wr[n // 3, n % 3], even_384[...]).astype(BF)
        return carry

    lax.fori_loop(0, 9, reorder, 0)
    for copy in halo:
        copy.wait()

    rim_l, rim_c = [], []
    for s in range(2):
        near = mm(rims[...], rim[s]).astype(BF)
        rim_l.append(jnp.concatenate([near[0:16], near[16:32], near[32:48]], axis=1))
        rim_c.append(jnp.concatenate([near[48:80], near[80:112, 0:64]], axis=1))
    for t in range(3):
        here = lc[t].reshape(64, 384)
        for j in range(3):
            wide = mm(lift[j], here)
            if j != 1:
                wide += mm(lift_rim[j // 2, t], rim_l[j // 2])
            sl[j, t] = wide.astype(BF).reshape(6, 16, 384)

    def fwd(i, total):
        for j in range(3):
            total += mm_nt(sl[j, :, pl.ds(i, 4)].reshape(192, 384), wrp[i, j])
        return total

    z_float = lax.fori_loop(0, 3, fwd, jnp.zeros((192, 192), F32)).astype(BF).astype(F32)
    gain = gain_v[...]
    inverse = lax.rsqrt(jnp.mean(z_float * z_float, axis=-1, keepdims=True) + EPSILON)
    normed = z_float * inverse
    scaled = normed * gain
    sigma = 1.0 / (1.0 + jnp.exp(-scaled))
    hidden = (scaled * sigma).astype(BF)
    hidden_t = mm_nt(even_192[...], hidden).astype(BF)

    for f in range(5):
        here = sc[1, f].reshape(96, 192)
        for s in range(2):
            moved = mm(cot[s], here) + mm(cot_rim[s, f], rim_c[s])
            sc[2 * s, f] = moved.astype(BF).reshape(6, 16, 192)

    def cot_view(a, i, j):
        return sc[2 - j, pl.ds(2 - a, 3), pl.ds(2 - i, 4)].reshape(192, 192)

    def planes(both, half, dst, at):
        dst[0, pl.ds(at, half)] = both[:half, :128]
        dst[1, pl.ds(at, half)] = jnp.concatenate([both[:half, 128:], both[half:, :64]], axis=1)
        dst[2, pl.ds(at, half)] = both[half:, 64:]

    def conv_tap(n, j):
        at = (n * 3 + j) * 96
        planes(mm(hidden_t, cot_view(n // 3, n % 3, j)), 96, fc, at if isinstance(n, int) else pl.multiple_of(at, 96))

    def conv_taps(n, carry):
        for j in range(3):
            conv_tap(n, j)
        return carry

    lane_row = lax.broadcasted_iota(jnp.int32, (8, 128), 0)

    def block_c(hh, i, t):
        at = (81 * (t * 8 + 4 * hh + i)) // 2
        spare = jnp.zeros((8, 128), F32)
        for q in range(3):
            spare = jnp.where(lane_row == q, fc[q, pl.ds(at + 40, 1)], spare)
        return jnp.concatenate([fc[q, pl.ds(at, 40)] for q in range(3)] + [spare], axis=0)

    def block_r(hh, i, t):
        at = 27 * (t * 8 + 4 * hh + i)
        return jnp.concatenate([fr[q, pl.ds(at, 32)] for q in range(3)], axis=0)

    parts = [
        (block_c, (0, 1)), (block_c, (3, 6)), (block_c, (2, 4, 5, 7)),
        (block_r, (0, 2, 4, 6)), (block_r, (1, 3, 5, 7)),
    ]

    def halves(p):
        tms = list(enumerate(parts[p][1]))
        return tms[: len(tms) // 2], tms[len(tms) // 2 :]

    def core_copy(p, o):
        bs, br = bufs[p][:2]
        i = (x + o) % 4
        return pltpu.make_async_remote_copy(
            src_ref=bs.at[i], dst_ref=br.at[i], send_sem=core_s.at[p * 4 + o],
            recv_sem=core_r.at[p * 4 + o], device_id=partner, device_id_type=MESH)

    def x_copy(p, m):
        xs, xr = bufs[p][2:4]
        return pltpu.make_async_remote_copy(
            src_ref=xs.at[m], dst_ref=xr.at[m], send_sem=x_s.at[p * 6 + m],
            recv_sem=x_r.at[p * 6 + m], device_id=peer_x(1 if m % 2 == 0 else 3), device_id_type=MESH)

    def core_send(p):
        block, tms = parts[p]
        bs = bufs[p][0]
        for o in (2, 1, 3, 0):
            i = (x + o) % 4
            for n, t in enumerate(tms):
                bs[i, n] = block(1 - h, i, t).astype(BF)
            core_copy(p, o).start()

    def x_fill(p, m, i, half, relayed):
        block = parts[p][0]
        _, br, xs, xr = bufs[p][:4]
        for k, (n, t) in enumerate(half):
            total = block(h, i, t) + br[i, n].astype(F32)
            if relayed:
                total += xr[m - 4, k].astype(F32)
            xs[m, k] = total.astype(BF)
        x_copy(p, m).start()

    def x_first(p):
        block, tms = parts[p]
        one, two = halves(p)
        br, ac = bufs[p][1], bufs[p][4]
        core_copy(p, 2).wait()
        x_fill(p, 0, (x + 2) % 4, one, False)
        x_fill(p, 1, (x + 2) % 4, two, False)
        core_copy(p, 1).wait()
        x_fill(p, 2, (x + 1) % 4, two, False)
        core_copy(p, 3).wait()
        x_fill(p, 3, (x + 3) % 4, one, False)
        core_copy(p, 0).wait()
        for n, t in enumerate(tms):
            ac[n] = block(h, x, t) + br[x, n].astype(F32)

    def x_second(p):
        one, two = halves(p)
        x_copy(p, 0).wait()
        x_fill(p, 4, (x + 1) % 4, one, True)
        x_copy(p, 1).wait()
        x_fill(p, 5, (x + 3) % 4, two, True)

    def y_copy(p, n):
        t = parts[p][1][n]
        ys, yr = y_bufs[p]
        return pltpu.make_async_remote_copy(
            src_ref=ys.at[n], dst_ref=yr.at[y], send_sem=y_s.at[p // 3 * 8 + t],
            recv_sem=y_r.at[p // 3 * 8 + y], device_id=(t, r, c), device_id_type=MESH)

    def y_send(p):
        xr, ac, ys = bufs[p][3], bufs[p][4], y_bufs[p][0]
        for m in range(2, 6):
            x_copy(p, m).wait()
        for half, one, two in zip(halves(p), (4, 5), (3, 2)):
            for k, (n, t) in enumerate(half):
                total = ac[n] + xr[one, k].astype(F32) + xr[two, k].astype(F32)
                ac[n] = total
                ys[n] = total.astype(BF)
        for n, t in enumerate(parts[p][1]):

            @pl.when(y != t)
            def _():
                y_copy(p, n).start()

    def y_wait_send(p):
        for n, t in enumerate(parts[p][1]):

            @pl.when(y != t)
            def _():
                y_copy(p, n).wait_send()

    def y_sum(p, dst):
        ac, yr = bufs[p][4], y_bufs[p][1]
        at = 0
        for n, t in enumerate(parts[p][1]):
            at = jnp.where(y == t, n + 1, at)

        @pl.when(at > 0)
        def _():
            total = ac[at - 1]
            for o in range(1, 8):
                k = (y + o) % 8
                pltpu.make_async_copy(yr.at[k], yr.at[k], y_r.at[p // 3 * 8 + k]).wait()
                total += yr[k].astype(F32)
            dst[...] = total.reshape(dst.shape)

    lax.fori_loop(0, 2, conv_taps, 0)
    conv_tap(2, 0)
    core_send(0)
    conv_tap(2, 1)
    conv_tap(2, 2)
    conv_taps(3, 0)
    lax.fori_loop(4, 9, conv_taps, 0)
    core_send(1)
    core_send(2)
    x_first(0)
    x_first(1)
    x_first(2)

    def back(n, total):
        a, i = n // 3, n % 3
        for j in range(3):
            total += mm_nt(cot_view(a, i, j), wc[a, i, j])
        return total

    hidden_grad = lax.fori_loop(0, 9, back, jnp.zeros((192, 192), F32))
    scaled_grad = hidden_grad * sigma * (1.0 + scaled * (1.0 - sigma))
    gain_local = jnp.sum(scaled_grad * normed, axis=0, keepdims=True)
    normed_grad = scaled_grad * gain
    delta = (
        inverse * (normed_grad - normed * jnp.mean(normed_grad * normed, axis=-1, keepdims=True))
    ).astype(BF)
    xd[:, 1:5] = delta.reshape(3, 4, 16, 192)
    rows_d = [
        Halo(xd.at[f3, 1], xd.at[f3, 5], 7, 0, -1, 0),
        Halo(xd.at[f3, 4], xd.at[f3, 0], 8, 0, 1, 0),
    ]
    for copy in rows_d:
        copy.start()

    tail = jnp.concatenate([gain_local[:, 128:], jnp.zeros((1, 64), F32)], axis=1)
    g_core[h] = jnp.where(lane_row == 0, gain_local[:, :128], jnp.where(lane_row == 1, tail, 0.0))

    def small(buf, at, ss, rs, n, to):
        return pltpu.make_async_remote_copy(
            src_ref=buf.at[at], dst_ref=buf.at[at], send_sem=ss.at[n], recv_sem=rs.at[n],
            device_id=to, device_id_type=MESH)

    g1 = small(g_core, h, gc_s, gc_r, 0, partner)
    g1.start()
    x_second(0)
    x_second(1)


    def lift_taps(n, carry):
        for j in range(3):
            at = pl.multiple_of((n * 3 + j) * 192, 192)
            view = sl[j, :, pl.ds(n, 4)].reshape(192, 384)
            planes(mm_tn(view, delta), 192, fr, at)
        return carry

    lax.fori_loop(0, 3, lift_taps, 0)
    core_send(3)
    core_send(4)
    for copy in rows_d:
        copy.wait()
    hs_d[...] = mm(edge_delta[...], xd[...].reshape(288, 192)).astype(BF)
    cols_d = [
        Halo(hs_d.at[pl.ds(0, 32)], rim_d.at[1], 9, 0, 0, -1),
        Halo(hs_d.at[pl.ds(32, 32)], rim_d.at[0], 10, 0, 0, 1),
    ]
    for copy in cols_d:
        copy.start()

    g1.wait()
    g_x[x] = g_core[0] + g_core[1]
    g2 = [small(g_x, x, gx_s, gx_r, o - 1, peer_x(o)) for o in range(1, 4)]
    for copy in g2:
        copy.start()

    x_first(3)
    x_first(4)
    x_second(2)
    y_send(0)
    y_send(1)
    x_second(3)
    for copy in g2:
        copy.wait()
    g_y[y] = (g_x[0] + g_x[1]) + (g_x[2] + g_x[3])
    g3 = [small(g_y, y, gy_s, gy_r, o - 1, dev(o)) for o in range(1, 8)]
    for copy in g3:
        copy.start()
    x_second(4)
    y_send(2)
    y_send(3)
    y_send(4)

    for copy in cols_d:
        copy.wait()

    for t in range(3):
        here = xd[t].reshape(96, 192)
        for j in range(3):
            moved = mm(pair[j], here)
            if j != 1:
                moved += mm(pair_rim[j // 2, t], rim_d[j // 2])
            sd[j, t] = moved.astype(BF).reshape(6, 16, 192)

    def unlift(i, total):
        for j in range(3):
            total += mm(sd[2 - j, :, pl.ds(2 - i, 4)].reshape(192, 192), wr[i, j])
        return total

    lifted_grad = lax.fori_loop(0, 3, unlift, jnp.zeros((192, 384), F32))
    gi_ref[...] = lifted_grad.reshape(3, 2, 4, 8, 384).sum(axis=2).astype(BF)


    for copy in g3:
        copy.wait()
    g_sum = g_y[0]
    for k in range(1, 8):
        g_sum += g_y[k]
    g_hi = g_sum.astype(BF).astype(F32)
    g_lo = g_sum - g_hi

    extra = jnp.concatenate([g_hi[0:2], g_lo[0:2], jnp.zeros((4, 128), F32)], axis=0)

    def fin_copy(n, q):
        to = (y, 4 * h + x, q)
        src, dst = ((ws_c, land_c), (ws_r, land_r))[n]
        remote_one = pltpu.make_async_remote_copy(
            src_ref=src.at[q], dst_ref=dst.at[z], send_sem=fin_s.at[n * 8 + q], recv_sem=fin_r.at[n * 8 + z],
            device_id=to, device_id_type=MESH)
        return remote_one, jnp.logical_and(to[1] == r, q == c)

    def fin_start(n, q):
        remote_one, own = fin_copy(n, q)
        src, dst = ((ws_c, land_c), (ws_r, land_r))[n]

        @pl.when(jnp.logical_not(own))
        def _():
            remote_one.start()

        @pl.when(own)
        def _():
            pltpu.make_async_copy(src.at[q], dst.at[z], fin_r.at[n * 8 + z]).start()

    for p in range(3):
        y_sum(p, sum_c)
    pw_c[...] = jnp.zeros((3, 48, 128), F32)
    for q in range(3):
        pw_c[q, 0:40] = sum_c[40 * q : 40 * q + 40]
        pw_c[q, 40:41] = sum_c[120 + q : 121 + q]
    for q in range(8):
        rows = [pw_c[k, 5 * q : 5 * q + 8] for k in range(3)]
        ws_c[q] = jnp.concatenate(rows + [extra], axis=0).astype(BF)
        fin_start(0, q)

    y_sum(3, pw_r)
    y_sum(4, pw_r)
    pack[...] = jnp.zeros((16, 128), F32)
    for q in range(8):
        low = (27 * q) // 8
        for k in range(3):
            pack[5 * k : 5 * k + 5] = pw_r[k, low : low + 5]
        ws_r[q] = pack[...].astype(BF)
        fin_start(1, q)

    def fin_sum(n):
        src, dst = ((ws_c, land_c), (ws_r, land_r))[n]
        total = jnp.zeros(dst.shape[1:], F32)
        for k in range(8):
            pltpu.make_async_copy(src.at[0], dst.at[k], fin_r.at[n * 8 + k]).wait()
            total += dst[k].astype(F32)
        return total

    flat_c[...] = jnp.zeros((24, 128), F32)
    flat_r[...] = jnp.zeros((24, 128), F32)
    total = fin_sum(0)
    og_ref[...] = total[24:26] + total[26:28]
    for k in range(3):
        for u in range(6):
            flat_c[3 * u + k : 3 * u + k + 1] = total[8 * k + u : 8 * k + u + 1]

    def cut(flat, off):
        lane = lax.broadcasted_iota(jnp.int32, (16, 128), 1)
        m, s = off // 128, off % 128
        turn = (128 - s) % 128
        one = pltpu.roll(flat[pl.ds(m, 16)], turn, 1)
        two = pltpu.roll(flat[pl.ds(m + 1, 16)], turn, 1)
        return jnp.where(lane < 128 - s, one, two)

    oc_ref[...] = cut(flat_c, 192 * (r % 2) + 24 * c)

    for p in range(5):
        y_wait_send(p)
    for n in range(2):
        for q in range(8):
            remote_one, own = fin_copy(n, q)

            @pl.when(jnp.logical_not(own))
            def _():
                remote_one.wait_send()

    total = fin_sum(1)
    for k in range(3):
        for u in range(5):
            flat_r[3 * u + k : 3 * u + k + 1] = total[5 * k + u : 5 * k + u + 1]
    or_ref[...] = cut(flat_r, 1296 * c - 384 * ((27 * c) // 8))


def hand_over(gi, oc, orr, og, gi_out, oc_out, or_out, og_out):
    gi_out[...], oc_out[...], or_out[...], og_out[...] = gi[...], oc[...], orr[...], og[...]


def local(latent, cotangent, resample_weight, conv_weight, norm_gain):
    vm = pl.BlockSpec(memory_space=pltpu.VMEM)
    far = pl.BlockSpec(memory_space=pltpu.HBM)
    consts = selectors()
    dma, V = pltpu.SemaphoreType.DMA, pltpu.VMEM

    def reduce_buffers(n, tms):
        return [
            V((4, tms, n, 128), BF), V((4, tms, n, 128), BF), V((6, tms // 2, n, 128), BF),
            V((6, tms // 2, n, 128), BF), V((tms, n, 128), F32),
        ]

    scratch = [V(a.shape, BF) for a in consts]
    scratch += [
        V((3, 2, 8, 384), BF), V((1, 192), F32), V((3, 3, 192, 384), BF), V((3, 3, 192, 384), BF),
        V((3, 3, 3, 192, 192), BF),
        V((3, 5, 6, 16, 192), BF), V((3, 4, 16, 384), BF),
        V((192, 128), BF), V((2, 128, 128), BF), V((64, 192), BF), V((2, 32, 192), BF),
        V((3, 3, 6, 16, 384), BF),
        V((3, 6, 16, 192), BF), V((3, 3, 6, 16, 192), BF),
        V((3, 2592 + 48, 128), F32), V((3, 1728 + 32, 128), F32),
        V((2, 8, 128), F32), V((4, 8, 128), F32), V((8, 8, 128), F32),
        V((128, 128), F32), V((3, 48, 128), F32), V((3, 32, 128), F32),
        V((8, 32, 128), BF), V((8, 16, 128), BF), V((8, 32, 128), BF), V((8, 16, 128), BF),
        V((16, 128), F32), V((24, 128), F32), V((24, 128), F32),
        dma((17,)), dma((23,)), dma((23,)), dma((20,)), dma((20,)), dma((30,)), dma((30,)), dma((16,)), dma((16,)),
        dma((16,)), dma((16,)), dma((1,)), dma((1,)), dma((3,)), dma((3,)), dma((7,)), dma((7,)),
        *reduce_buffers(128, 2), *reduce_buffers(128, 2), *reduce_buffers(128, 4),
        *reduce_buffers(96, 4), *reduce_buffers(96, 4),
        V((2, 128, 128), BF), V((2, 128, 128), BF), V((4, 128, 128), BF), V((4, 96, 128), BF), V((4, 96, 128), BF), V((8, 128, 128), BF), V((8, 96, 128), BF),
    ]
    gi, oc, orr, og = pl.pallas_call(
        kernel,
        out_shape=[
            jax.ShapeDtypeStruct((3, 2, 8, 384), BF),
            jax.ShapeDtypeStruct((16, 128), F32),
            jax.ShapeDtypeStruct((16, 128), F32),
            jax.ShapeDtypeStruct((2, 128), F32),
        ],
        in_specs=[far] * (5 + len(consts)),
        out_specs=[vm] * 4,
        scratch_shapes=scratch,
        compiler_params=pltpu.CompilerParams(
            collective_id=0, has_side_effects=True, vmem_limit_bytes=56 * 2**20
        ),
        cost_estimate=pl.CostEstimate(flops=1_600_000_000, bytes_accessed=5_000_000, transcendentals=40_000),
    )(latent, cotangent, norm_gain.reshape(1, 192), jnp.swapaxes(resample_weight, 2, 3), conv_weight, *consts)
    shapes = [jax.ShapeDtypeStruct(a.shape, a.dtype) for a in (gi, oc, orr, og)]
    gi, oc, orr, og = pl.pallas_call(
        hand_over, out_shape=shapes, in_specs=[vm] * 4, out_specs=[vm] * 4
    )(gi, oc, orr, og)
    return gi, orr.reshape(-1)[:1296], oc.reshape(-1)[:1944], og.reshape(-1)[:192]


def solution(mesh):
    in_specs = (P("tm", "rows", "cols", None), P("tm", "rows", "cols", None), P(), P(), P())
    out_specs = (
        P("tm", "rows", "cols", None),
        P(("tm", "rows", "cols")),
        P(("tm", "rows", "cols")),
        P(),
    )
    return jax.shard_map(local, mesh=mesh, in_specs=in_specs, out_specs=out_specs, check_vma=False)
```

```python
import functools

import jax
import jax.numpy as jnp
import numpy as np
from jax import lax
from jax.experimental import pallas as pl
from jax.experimental.pallas import tpu as pltpu
from jax.sharding import PartitionSpec as P

EPSILON = 1e-06
MESH = pl.DeviceIdType.MESH
BF = jnp.bfloat16
F32 = jnp.float32


def selectors():
    low = [0, 1, 1, 2, 2, 3]

    def zeros(*dims):
        return np.zeros(dims, np.float32)

    widen = zeros(96, 48)
    for t in range(3):
        for l in range(2):
            for c in range(16):
                widen[t * 32 + l * 16 + c, t * 16 + l * 8 + c // 2] = 1
    even_192, even_384 = zeros(192, 192), zeros(384, 384)
    for u in range(96):
        even_192[u, 2 * u] = even_192[96 + u, 2 * u + 1] = 1
    for u in range(192):
        even_384[2 * u, u] = even_384[2 * u + 1, 192 + u] = 1
    lift, lift_rim = zeros(3, 96, 64), zeros(2, 3, 96, 16)
    cot, cot_rim = zeros(2, 96, 96), zeros(2, 5, 96, 32)
    pair, pair_rim = zeros(3, 96, 96), zeros(2, 3, 96, 32)

    for row in range(6):
        for c in range(16):
            out = row * 16 + c
            par = row * 16 + (c % 2) * 8 + c // 2
            for j in range(3):
                at = c + j - 1
                if 0 <= at < 16:
                    lift[j, out, low[row] * 16 + at] = 1
                    pair[j, par, row * 16 + at] = 1
                    if j != 1:
                        cot[j // 2, out, row * 16 + at] = 1
                else:
                    side = j // 2
                    for f in range(5):
                        cot_rim[side, f, out, f * 6 + row] = 1
                    for f in range(3):
                        lift_rim[side, f, out, f * 4 + low[row]] = 1
                        pair_rim[side, f, par, f * 6 + row] = 1
    edge_delta, edges, rims = zeros(64, 288), zeros(192, 528), zeros(112, 128)
    for side, col in ((0, 0), (1, 15)):
        for n in range(18):
            edge_delta[side * 32 + n, n * 16 + col] = 1
        for chunks, rows, src, at, corner in ((3, 2, 0, 0, 0), (2, 4, 144, 18, 9)):
            wide, at_col = (8, col // 2) if rows == 2 else (16, col)
            for q in range(chunks):
                for t in range(3):
                    here = src + (q * 3 + t) * rows * wide + at_col
                    for row in range(rows):
                        edges[side * 96 + at + (q * 3 + t) * rows + row, here + row * wide] = 1
                        if rows == 4 and t < 2:
                            edges[side * 96 + 80 + q * 8 + t * 4 + row, here + row * wide] = 1
                    edges[side * 96 + 48 + corner + q * 3 + t, here] = 1
                    edges[side * 96 + 64 + corner + q * 3 + t, here + (rows - 1) * wide] = 1
    for t in range(3):
        for q in range(3):
            rims[q * 16 + t * 4, 48 + q * 3 + t] = rims[q * 16 + t * 4 + 3, 64 + q * 3 + t] = 1
            for row in range(2):
                rims[q * 16 + t * 4 + 1 + row, q * 6 + t * 2 + row] = 1
        for q in range(2):
            for f, base, up, down in ((t, 18 + q * 12, 48, 64), (t + 3, 80 + q * 8, 96, 112)):
                if f < 5:
                    at = 48 + q * 32 + f * 6
                    rims[at, up + 9 + q * 3 + t] = rims[at + 5, down + 9 + q * 3 + t] = 1
                    for row in range(4):
                        rims[at + 1 + row, base + t * 4 + row] = 1
    parts = (edges, even_384, widen, rims, even_192, lift, lift_rim, cot, cot_rim, pair, pair_rim, edge_delta)
    return [jnp.asarray(p, BF) for p in parts]


def mm(a, b):
    return jnp.dot(a, b, preferred_element_type=F32)


def mm_nt(a, b):
    return lax.dot_general(a, b, (((1,), (1,)), ((), ())), preferred_element_type=F32)


def mm_tn(a, b):
    return lax.dot_general(a, b, (((0,), (0,)), ((), ())), preferred_element_type=F32)


def kernel(*refs):
    (latent_hbm, cot_hbm, gain_hbm, wr_hbm, wc_hbm), refs = refs[:5], refs[5:]
    const_hbm, (gi_ref, oc_ref, or_ref, og_ref), refs = refs[:12], refs[12:16], refs[16:]
    consts, refs = refs[:12], refs[12:]
    (edges, even_384, widen, rims, even_192, lift, lift_rim, cot, cot_rim, pair, pair_rim, edge_delta) = consts
    (
        latv, gain_v, wr, wrp, wc, sc, lc, hs, rim, hs_d, rim_d, sl, xd, sd, fc, fr,
        g_core, g_x, g_y, sum_c, pw_c, pw_r, ws_c, ws_r, land_c, land_r, pack, flat_c, flat_r,
        load_sem, ssem, rsem, core_s, core_r, x_s, x_r, y_s, y_r, fin_s, fin_r,
        gc_s, gc_r, gx_s, gx_r, gy_s, gy_r,
    ), refs = refs[:46], refs[46:]
    bufs = [refs[5 * p : 5 * p + 5] for p in range(5)]
    yr_c, yr_r = refs[30:32]
    y_bufs = [(refs[25 + p], yr_c if p < 3 else yr_r) for p in range(5)]

    y, r, c = lax.axis_index("tm"), lax.axis_index("rows"), lax.axis_index("cols")
    h, zl = r % 2, r // 2
    x, zh = c % 4, c // 4
    z = zh * 4 + zl

    def dev(dy=0, dr=0, dc=0):
        return ((y + dy + 8) % 8, (r + dr + 8) % 8, (c + dc + 8) % 8)

    partner = (y, zl * 2 + 1 - h, c)

    def peer_x(o):
        return (y, r, zh * 4 + (x + o) % 4)

    f3, f2, late = pl.ds(0, 3), pl.ds(0, 2), pl.ds(3, 2)
    targets = [(latent_hbm, latv), (cot_hbm, sc.at[1, f3, pl.ds(1, 4)])]
    targets += list(zip(const_hbm, consts)) + [(gain_hbm, gain_v), (wr_hbm, wr), (wc_hbm, wc)]
    loads = [pltpu.make_async_copy(a, b, load_sem.at[n]) for n, (a, b) in enumerate(targets)]
    for copy in loads[:5]:
        copy.start()

    bar = pltpu.get_barrier_semaphore()
    sources = [dev(dy, dr, dc) for dc in (1, -1, 0) for dr in (-1, 0, 1) for dy in (0, 1) if (dy, dr, dc) != (0, 0, 0)]
    sources += [partner] + [peer_x(o) for o in range(1, 4)] + [dev(o) for o in range(1, 8)]
    for d in sources:
        pl.semaphore_signal(bar, inc=1, device_id=d, device_id_type=MESH)
    for q in range(8):
        src = (y, 2 * (q % 4) + r // 4, (q // 4) * 4 + r % 4)

        @pl.when(jnp.logical_or(src[1] != r, src[2] != c))
        def _():
            pl.semaphore_signal(bar, inc=1, device_id=src, device_id_type=MESH)

    mine = jnp.where(r == 4 * h + x, 1, 0)
    for copy in loads[:4]:
        copy.wait()

    own_low = mm(latv[...].astype(F32).reshape(48, 384).astype(BF), even_384[...]).astype(BF)
    own_cot = sc[1, 0:3, 1:5].reshape(192, 192)
    chunks = [own_low[:, 0:128], own_low[:, 128:256], own_low[:, 256:384], own_cot[:, 0:128]]
    chunks += [jnp.concatenate([own_cot[:, 128:192], jnp.zeros((192, 64), BF)], axis=1)]
    hs[...] = mm(edges[...], jnp.concatenate(chunks, axis=0)).astype(BF)

    pl.semaphore_wait(bar, len(sources) + 8 - mine)

    def inside(dy, dr, dc):
        ok = y >= 0
        for at, d in ((y, dy), (r, dr), (c, dc)):
            if d:
                ok = jnp.logical_and(ok, at < 7 if d > 0 else at > 0)
        return ok

    class Halo:
        def __init__(self, src, dst, n, *to):
            self.to, self.back = inside(*to), inside(*[-d for d in to])
            self.copy = pltpu.make_async_remote_copy(
                src_ref=src, dst_ref=dst, send_sem=ssem.at[n], recv_sem=rsem.at[n],
                device_id=dev(*to), device_id_type=MESH,
            )

        def start(self):
            pl.when(self.to)(self.copy.start)

        def wait(self):
            pl.when(self.to)(self.copy.wait_send)
            pl.when(self.back)(self.copy.wait_recv)

    halo = []
    for s, dc in ((0, -1), (1, 1)):
        tiles = ((0, 48, 0, 0, 0), (64, 16, 48, 0, 1), (48, 16, 64, 0, -1), (80, 16, 80, -1, 0), (64, 16, 96, -1, 1), (48, 16, 112, -1, -1))
        for n, (src, rows, dst, dy, dr) in enumerate(tiles):
            halo.append(Halo(hs.at[pl.ds(96 * s + src, rows)], rim.at[1 - s, pl.ds(dst, rows)], 11 + 6 * s + n, dy, dr, dc))
    for copy in halo:
        copy.start()
    loads[4].wait()
    lc[:, 1:3] = mm(widen[...], own_low).astype(BF).reshape(3, 2, 16, 384)
    halo += [
        Halo(lc.at[f3, 1], lc.at[f3, 3], 5, 0, -1, 0),
        Halo(lc.at[f3, 2], lc.at[f3, 0], 6, 0, 1, 0),
        Halo(sc.at[1, f3, 1], sc.at[1, f3, 5], 0, 0, -1, 0),
        Halo(sc.at[1, f3, 4], sc.at[1, f3, 0], 1, 0, 1, 0),
        Halo(sc.at[1, f2, pl.ds(1, 4)], sc.at[1, late, pl.ds(1, 4)], 2, -1, 0, 0),
        Halo(sc.at[1, f2, 1], sc.at[1, late, 5], 3, -1, -1, 0),
        Halo(sc.at[1, f2, 4], sc.at[1, late, 0], 4, -1, 1, 0),
    ]
    for copy in halo[12:] + loads[5:]:
        copy.start()

    @pl.when(r == 0)
    def _():
        sc[1, :, 0] = jnp.zeros((5, 16, 192), BF)
        lc[:, 0] = jnp.zeros((3, 16, 384), BF)
        xd[:, 0] = jnp.zeros((3, 16, 192), BF)
        for n in (48, 96):
            rim[:, n : n + 16] = jnp.zeros((2, 16, 128), BF)

    @pl.when(r == 7)
    def _():
        sc[1, :, 5] = jnp.zeros((5, 16, 192), BF)
        lc[:, 3] = jnp.zeros((3, 16, 384), BF)
        xd[:, 5] = jnp.zeros((3, 16, 192), BF)
        for n in (64, 112):
            rim[:, n : n + 16] = jnp.zeros((2, 16, 128), BF)

    @pl.when(y == 7)
    def _():
        sc[1, 3:5] = jnp.zeros((2, 6, 16, 192), BF)
        rim[:, 80:128] = jnp.zeros((2, 48, 128), BF)

    @pl.when(c == 0)
    def _():
        rim[0] = jnp.zeros((128, 128), BF)
        rim_d[0] = jnp.zeros((32, 192), BF)

    @pl.when(c == 7)
    def _():
        rim[1] = jnp.zeros((128, 128), BF)
        rim_d[1] = jnp.zeros((32, 192), BF)

    for copy in loads[5:]:
        copy.wait()

    def reorder(n, carry):
        wrp[n // 3, n % 3] = mm(wr[n // 3, n % 3], even_384[...]).astype(BF)
        return carry

    lax.fori_loop(0, 9, reorder, 0)
    for copy in halo:
        copy.wait()

    rim_l, rim_c = [], []
    for s in range(2):
        near = mm(rims[...], rim[s]).astype(BF)
        rim_l.append(jnp.concatenate([near[0:16], near[16:32], near[32:48]], axis=1))
        rim_c.append(jnp.concatenate([near[48:80], near[80:112, 0:64]], axis=1))
    for t in range(3):
        here = lc[t].reshape(64, 384)
        for j in range(3):
            wide = mm(lift[j], here)
            if j != 1:
                wide += mm(lift_rim[j // 2, t], rim_l[j // 2])
            sl[j, t] = wide.astype(BF).reshape(6, 16, 384)

    def fwd(i, total):
        for j in range(3):
            total += mm_nt(sl[j, :, pl.ds(i, 4)].reshape(192, 384), wrp[i, j])
        return total

    z_float = lax.fori_loop(0, 3, fwd, jnp.zeros((192, 192), F32)).astype(BF).astype(F32)
    gain = gain_v[...]
    inverse = lax.rsqrt(jnp.mean(z_float * z_float, axis=-1, keepdims=True) + EPSILON)
    normed = z_float * inverse
    scaled = normed * gain
    sigma = 1.0 / (1.0 + jnp.exp(-scaled))
    hidden = (scaled * sigma).astype(BF)
    hidden_t = mm_nt(even_192[...], hidden).astype(BF)

    for f in range(5):
        here = sc[1, f].reshape(96, 192)
        for s in range(2):
            moved = mm(cot[s], here) + mm(cot_rim[s, f], rim_c[s])
            sc[2 * s, f] = moved.astype(BF).reshape(6, 16, 192)

    def cot_view(a, i, j):
        return sc[2 - j, pl.ds(2 - a, 3), pl.ds(2 - i, 4)].reshape(192, 192)

    def planes(both, half, dst, at):
        dst[0, pl.ds(at, half)] = both[:half, :128]
        dst[1, pl.ds(at, half)] = jnp.concatenate([both[:half, 128:], both[half:, :64]], axis=1)
        dst[2, pl.ds(at, half)] = both[half:, 64:]

    def conv_tap(n, j):
        at = (n * 3 + j) * 96
        planes(mm(hidden_t, cot_view(n // 3, n % 3, j)), 96, fc, at if isinstance(n, int) else pl.multiple_of(at, 96))

    def conv_taps(n, carry):
        for j in range(3):
            conv_tap(n, j)
        return carry

    lane_row = lax.broadcasted_iota(jnp.int32, (8, 128), 0)

    def block_c(hh, i, t):
        at = (81 * (t * 8 + 4 * hh + i)) // 2
        spare = jnp.zeros((8, 128), F32)
        for q in range(3):
            spare = jnp.where(lane_row == q, fc[q, pl.ds(at + 40, 1)], spare)
        return jnp.concatenate([fc[q, pl.ds(at, 40)] for q in range(3)] + [spare], axis=0)

    def block_r(hh, i, t):
        at = 27 * (t * 8 + 4 * hh + i)
        return jnp.concatenate([fr[q, pl.ds(at, 32)] for q in range(3)], axis=0)

    parts = [
        (block_c, (0, 1)), (block_c, (3, 6)), (block_c, (2, 4, 5, 7)),
        (block_r, (0, 2, 4, 6)), (block_r, (1, 3, 5, 7)),
    ]

    def halves(p):
        tms = list(enumerate(parts[p][1]))
        return tms[: len(tms) // 2], tms[len(tms) // 2 :]

    def core_copy(p, o):
        bs, br = bufs[p][:2]
        i = (x + o) % 4
        return pltpu.make_async_remote_copy(
            src_ref=bs.at[i], dst_ref=br.at[i], send_sem=core_s.at[p * 4 + o],
            recv_sem=core_r.at[p * 4 + o], device_id=partner, device_id_type=MESH)

    def x_copy(p, m):
        xs, xr = bufs[p][2:4]
        return pltpu.make_async_remote_copy(
            src_ref=xs.at[m], dst_ref=xr.at[m], send_sem=x_s.at[p * 6 + m],
            recv_sem=x_r.at[p * 6 + m], device_id=peer_x(1 if m % 2 == 0 else 3), device_id_type=MESH)

    def core_send(p):
        block, tms = parts[p]
        bs = bufs[p][0]
        for o in (2, 1, 3, 0):
            i = (x + o) % 4
            for n, t in enumerate(tms):
                bs[i, n] = block(1 - h, i, t).astype(BF)
            core_copy(p, o).start()

    def x_fill(p, m, i, half, relayed):
        block = parts[p][0]
        _, br, xs, xr = bufs[p][:4]
        for k, (n, t) in enumerate(half):
            total = block(h, i, t) + br[i, n].astype(F32)
            if relayed:
                total += xr[m - 4, k].astype(F32)
            xs[m, k] = total.astype(BF)
        x_copy(p, m).start()

    def x_first(p):
        block, tms = parts[p]
        one, two = halves(p)
        br, ac = bufs[p][1], bufs[p][4]
        core_copy(p, 2).wait()
        x_fill(p, 0, (x + 2) % 4, one, False)
        x_fill(p, 1, (x + 2) % 4, two, False)
        core_copy(p, 1).wait()
        x_fill(p, 2, (x + 1) % 4, two, False)
        core_copy(p, 3).wait()
        x_fill(p, 3, (x + 3) % 4, one, False)
        core_copy(p, 0).wait()
        for n, t in enumerate(tms):
            ac[n] = block(h, x, t) + br[x, n].astype(F32)

    def x_second(p):
        one, two = halves(p)
        x_copy(p, 0).wait()
        x_fill(p, 4, (x + 1) % 4, one, True)
        x_copy(p, 1).wait()
        x_fill(p, 5, (x + 3) % 4, two, True)

    def y_copy(p, n):
        t = parts[p][1][n]
        ys, yr = y_bufs[p]
        return pltpu.make_async_remote_copy(
            src_ref=ys.at[n], dst_ref=yr.at[y], send_sem=y_s.at[p // 3 * 8 + t],
            recv_sem=y_r.at[p // 3 * 8 + y], device_id=(t, r, c), device_id_type=MESH)

    def y_send(p):
        xr, ac, ys = bufs[p][3], bufs[p][4], y_bufs[p][0]
        for m in range(2, 6):
            x_copy(p, m).wait()
        for half, one, two in zip(halves(p), (4, 5), (3, 2)):
            for k, (n, t) in enumerate(half):
                total = ac[n] + xr[one, k].astype(F32) + xr[two, k].astype(F32)
                ac[n] = total
                ys[n] = total.astype(BF)
        for n, t in enumerate(parts[p][1]):

            @pl.when(y != t)
            def _():
                y_copy(p, n).start()

    def y_wait_send(p):
        for n, t in enumerate(parts[p][1]):

            @pl.when(y != t)
            def _():
                y_copy(p, n).wait_send()

    def y_sum(p, dst):
        ac, yr = bufs[p][4], y_bufs[p][1]
        at = 0
        for n, t in enumerate(parts[p][1]):
            at = jnp.where(y == t, n + 1, at)

        @pl.when(at > 0)
        def _():
            total = ac[at - 1]
            for o in range(1, 8):
                k = (y + o) % 8
                pltpu.make_async_copy(yr.at[k], yr.at[k], y_r.at[p // 3 * 8 + k]).wait()
                total += yr[k].astype(F32)
            dst[...] = total.reshape(dst.shape)

    lax.fori_loop(0, 2, conv_taps, 0)
    conv_tap(2, 0)
    core_send(0)
    conv_tap(2, 1)
    conv_tap(2, 2)
    conv_taps(3, 0)
    lax.fori_loop(4, 9, conv_taps, 0)
    core_send(1)
    core_send(2)
    x_first(0)
    x_first(1)
    x_first(2)

    def back(n, total):
        a, i = n // 3, n % 3
        for j in range(3):
            total += mm_nt(cot_view(a, i, j), wc[a, i, j])
        return total

    hidden_grad = lax.fori_loop(0, 9, back, jnp.zeros((192, 192), F32))
    scaled_grad = hidden_grad * sigma * (1.0 + scaled * (1.0 - sigma))
    gain_local = jnp.sum(scaled_grad * normed, axis=0, keepdims=True)
    normed_grad = scaled_grad * gain
    delta = (
        inverse * (normed_grad - normed * jnp.mean(normed_grad * normed, axis=-1, keepdims=True))
    ).astype(BF)
    xd[:, 1:5] = delta.reshape(3, 4, 16, 192)
    rows_d = [
        Halo(xd.at[f3, 1], xd.at[f3, 5], 7, 0, -1, 0),
        Halo(xd.at[f3, 4], xd.at[f3, 0], 8, 0, 1, 0),
    ]
    for copy in rows_d:
        copy.start()

    tail = jnp.concatenate([gain_local[:, 128:], jnp.zeros((1, 64), F32)], axis=1)
    g_core[h] = jnp.where(lane_row == 0, gain_local[:, :128], jnp.where(lane_row == 1, tail, 0.0))

    def small(buf, at, ss, rs, n, to):
        return pltpu.make_async_remote_copy(
            src_ref=buf.at[at], dst_ref=buf.at[at], send_sem=ss.at[n], recv_sem=rs.at[n],
            device_id=to, device_id_type=MESH)

    g1 = small(g_core, h, gc_s, gc_r, 0, partner)
    g1.start()
    x_second(0)
    x_second(1)


    def lift_taps(n, carry):
        for j in range(3):
            at = pl.multiple_of((n * 3 + j) * 192, 192)
            view = sl[j, :, pl.ds(n, 4)].reshape(192, 384)
            planes(mm_tn(view, delta), 192, fr, at)
        return carry

    lax.fori_loop(0, 3, lift_taps, 0)
    core_send(3)
    core_send(4)
    for copy in rows_d:
        copy.wait()
    hs_d[...] = mm(edge_delta[...], xd[...].reshape(288, 192)).astype(BF)
    cols_d = [
        Halo(hs_d.at[pl.ds(0, 32)], rim_d.at[1], 9, 0, 0, -1),
        Halo(hs_d.at[pl.ds(32, 32)], rim_d.at[0], 10, 0, 0, 1),
    ]
    for copy in cols_d:
        copy.start()

    g1.wait()
    g_x[x] = g_core[0] + g_core[1]
    g2 = [small(g_x, x, gx_s, gx_r, o - 1, peer_x(o)) for o in range(1, 4)]
    for copy in g2:
        copy.start()

    x_first(3)
    x_second(2)
    x_first(4)
    y_send(0)
    y_send(1)
    x_second(3)
    for copy in g2:
        copy.wait()
    g_y[y] = (g_x[0] + g_x[1]) + (g_x[2] + g_x[3])
    g3 = [small(g_y, y, gy_s, gy_r, o - 1, dev(o)) for o in range(1, 8)]
    for copy in g3:
        copy.start()
    x_second(4)
    y_send(2)
    y_send(3)
    y_send(4)

    for copy in cols_d:
        copy.wait()

    for t in range(3):
        here = xd[t].reshape(96, 192)
        for j in range(3):
            moved = mm(pair[j], here)
            if j != 1:
                moved += mm(pair_rim[j // 2, t], rim_d[j // 2])
            sd[j, t] = moved.astype(BF).reshape(6, 16, 192)

    def unlift(i, total):
        for j in range(3):
            total += mm(sd[2 - j, :, pl.ds(2 - i, 4)].reshape(192, 192), wr[i, j])
        return total

    lifted_grad = lax.fori_loop(0, 3, unlift, jnp.zeros((192, 384), F32))
    gi_ref[...] = lifted_grad.reshape(3, 2, 4, 8, 384).sum(axis=2).astype(BF)


    for copy in g3:
        copy.wait()
    g_sum = g_y[0]
    for k in range(1, 8):
        g_sum += g_y[k]
    g_hi = g_sum.astype(BF).astype(F32)
    g_lo = g_sum - g_hi

    extra = jnp.concatenate([g_hi[0:2], g_lo[0:2], jnp.zeros((4, 128), F32)], axis=0)

    def fin_copy(n, q):
        to = (y, 4 * h + x, q)
        src, dst = ((ws_c, land_c), (ws_r, land_r))[n]
        remote_one = pltpu.make_async_remote_copy(
            src_ref=src.at[q], dst_ref=dst.at[z], send_sem=fin_s.at[n * 8 + q], recv_sem=fin_r.at[n * 8 + z],
            device_id=to, device_id_type=MESH)
        return remote_one, jnp.logical_and(to[1] == r, q == c)

    def fin_start(n, q):
        remote_one, own = fin_copy(n, q)
        src, dst = ((ws_c, land_c), (ws_r, land_r))[n]

        @pl.when(jnp.logical_not(own))
        def _():
            remote_one.start()

        @pl.when(own)
        def _():
            pltpu.make_async_copy(src.at[q], dst.at[z], fin_r.at[n * 8 + z]).start()

    for p in range(3):
        y_sum(p, sum_c)
    pw_c[...] = jnp.zeros((3, 48, 128), F32)
    for q in range(3):
        pw_c[q, 0:40] = sum_c[40 * q : 40 * q + 40]
        pw_c[q, 40:41] = sum_c[120 + q : 121 + q]
    for q in range(8):
        rows = [pw_c[k, 5 * q : 5 * q + 8] for k in range(3)]
        ws_c[q] = jnp.concatenate(rows + [extra], axis=0).astype(BF)
        fin_start(0, q)

    y_sum(3, pw_r)
    y_sum(4, pw_r)
    pack[...] = jnp.zeros((16, 128), F32)
    for q in range(8):
        low = (27 * q) // 8
        for k in range(3):
            pack[5 * k : 5 * k + 5] = pw_r[k, low : low + 5]
        ws_r[q] = pack[...].astype(BF)
        fin_start(1, q)

    def fin_sum(n):
        src, dst = ((ws_c, land_c), (ws_r, land_r))[n]
        total = jnp.zeros(dst.shape[1:], F32)
        for k in range(8):
            pltpu.make_async_copy(src.at[0], dst.at[k], fin_r.at[n * 8 + k]).wait()
            total += dst[k].astype(F32)
        return total

    flat_c[...] = jnp.zeros((24, 128), F32)
    flat_r[...] = jnp.zeros((24, 128), F32)
    total = fin_sum(0)
    og_ref[...] = total[24:26] + total[26:28]
    for k in range(3):
        for u in range(6):
            flat_c[3 * u + k : 3 * u + k + 1] = total[8 * k + u : 8 * k + u + 1]

    def cut(flat, off):
        lane = lax.broadcasted_iota(jnp.int32, (16, 128), 1)
        m, s = off // 128, off % 128
        turn = (128 - s) % 128
        one = pltpu.roll(flat[pl.ds(m, 16)], turn, 1)
        two = pltpu.roll(flat[pl.ds(m + 1, 16)], turn, 1)
        return jnp.where(lane < 128 - s, one, two)

    oc_ref[...] = cut(flat_c, 192 * (r % 2) + 24 * c)

    for p in range(5):
        y_wait_send(p)
    for n in range(2):
        for q in range(8):
            remote_one, own = fin_copy(n, q)

            @pl.when(jnp.logical_not(own))
            def _():
                remote_one.wait_send()

    total = fin_sum(1)
    for k in range(3):
        for u in range(5):
            flat_r[3 * u + k : 3 * u + k + 1] = total[5 * k + u : 5 * k + u + 1]
    or_ref[...] = cut(flat_r, 1296 * c - 384 * ((27 * c) // 8))


def hand_over(gi, oc, orr, og, gi_out, oc_out, or_out, og_out):
    gi_out[...], oc_out[...], or_out[...], og_out[...] = gi[...], oc[...], orr[...], og[...]


def local(latent, cotangent, resample_weight, conv_weight, norm_gain):
    vm = pl.BlockSpec(memory_space=pltpu.VMEM)
    far = pl.BlockSpec(memory_space=pltpu.HBM)
    consts = selectors()
    dma, V = pltpu.SemaphoreType.DMA, pltpu.VMEM

    def reduce_buffers(n, tms):
        return [
            V((4, tms, n, 128), BF), V((4, tms, n, 128), BF), V((6, tms // 2, n, 128), BF),
            V((6, tms // 2, n, 128), BF), V((tms, n, 128), F32),
        ]

    scratch = [V(a.shape, BF) for a in consts]
    scratch += [
        V((3, 2, 8, 384), BF), V((1, 192), F32), V((3, 3, 192, 384), BF), V((3, 3, 192, 384), BF),
        V((3, 3, 3, 192, 192), BF),
        V((3, 5, 6, 16, 192), BF), V((3, 4, 16, 384), BF),
        V((192, 128), BF), V((2, 128, 128), BF), V((64, 192), BF), V((2, 32, 192), BF),
        V((3, 3, 6, 16, 384), BF),
        V((3, 6, 16, 192), BF), V((3, 3, 6, 16, 192), BF),
        V((3, 2592 + 48, 128), F32), V((3, 1728 + 32, 128), F32),
        V((2, 8, 128), F32), V((4, 8, 128), F32), V((8, 8, 128), F32),
        V((128, 128), F32), V((3, 48, 128), F32), V((3, 32, 128), F32),
        V((8, 32, 128), BF), V((8, 16, 128), BF), V((8, 32, 128), BF), V((8, 16, 128), BF),
        V((16, 128), F32), V((24, 128), F32), V((24, 128), F32),
        dma((17,)), dma((23,)), dma((23,)), dma((20,)), dma((20,)), dma((30,)), dma((30,)), dma((16,)), dma((16,)),
        dma((16,)), dma((16,)), dma((1,)), dma((1,)), dma((3,)), dma((3,)), dma((7,)), dma((7,)),
        *reduce_buffers(128, 2), *reduce_buffers(128, 2), *reduce_buffers(128, 4),
        *reduce_buffers(96, 4), *reduce_buffers(96, 4),
        V((2, 128, 128), BF), V((2, 128, 128), BF), V((4, 128, 128), BF), V((4, 96, 128), BF), V((4, 96, 128), BF), V((8, 128, 128), BF), V((8, 96, 128), BF),
    ]
    gi, oc, orr, og = pl.pallas_call(
        kernel,
        out_shape=[
            jax.ShapeDtypeStruct((3, 2, 8, 384), BF),
            jax.ShapeDtypeStruct((16, 128), F32),
            jax.ShapeDtypeStruct((16, 128), F32),
            jax.ShapeDtypeStruct((2, 128), F32),
        ],
        in_specs=[far] * (5 + len(consts)),
        out_specs=[vm] * 4,
        scratch_shapes=scratch,
        compiler_params=pltpu.CompilerParams(
            collective_id=0, has_side_effects=True, vmem_limit_bytes=56 * 2**20
        ),
        cost_estimate=pl.CostEstimate(flops=1_600_000_000, bytes_accessed=5_000_000, transcendentals=40_000),
    )(latent, cotangent, norm_gain.reshape(1, 192), jnp.swapaxes(resample_weight, 2, 3), conv_weight, *consts)
    shapes = [jax.ShapeDtypeStruct(a.shape, a.dtype) for a in (gi, oc, orr, og)]
    gi, oc, orr, og = pl.pallas_call(
        hand_over, out_shape=shapes, in_specs=[vm] * 4, out_specs=[vm] * 4
    )(gi, oc, orr, og)
    return gi, orr.reshape(-1)[:1296], oc.reshape(-1)[:1944], og.reshape(-1)[:192]


def solution(mesh):
    in_specs = (P("tm", "rows", "cols", None), P("tm", "rows", "cols", None), P(), P(), P())
    out_specs = (
        P("tm", "rows", "cols", None),
        P(("tm", "rows", "cols")),
        P(("tm", "rows", "cols")),
        P(),
    )
    return jax.shard_map(local, mesh=mesh, in_specs=in_specs, out_specs=out_specs, check_vma=False)
```
